32 devices in a mesh: grp: 2 (over y), mem: 16 (over z, x, core).
Axes of the slice: x: 2, y: 2, z: 4, core: 2. Of those that a mesh axis runs over, the one named last changes fastest.
Arguments:
- user_factors: bfloat16 [32768, 256], P(('grp', 'mem')), may hold values from -1.5 to 1.5
- item_factors: bfloat16 [512, 256], P('mem'), may hold values from -1.5 to 1.5
- link_weights: bfloat16 [4096, 256], replicated, may hold values from -0.09375 to 0.09375
- item_feat: bfloat16 [16, 32, 4096], P('mem', 'grp'), may hold values from -6 to 6
- tile_values: bfloat16 [768, 128, 128], P(('grp', 'mem')), may hold values from -6 to 6
- tile_scale: float32 [768], P(('grp', 'mem')), may hold values from 0.25 to 2
- tile_place: int32 [768], P(('grp', 'mem')), may hold values from 0 to 31, as said below
- tile_count: int32 [32], P(('grp', 'mem')), may hold values from 1 to 24, as said below
- user_noise: bfloat16 [32768, 256], P(('grp', 'mem')), may hold values from -6 to 6
- item_noise: bfloat16 [16, 32, 256], P('mem', 'grp'), may hold values from -6 to 6
- link_noise: bfloat16 [4096, 256], P(('grp', 'mem')), may hold values from -6 to 6
Outputs:
- new_users: float32 [32768, 256], P(('grp', 'mem'))
- new_items: float32 [16, 32, 256], P('mem', 'grp')
- new_link: float32 [4096, 256], P(('grp', 'mem'))
The draws below stay inside these ranges and needn't reach their ends.
Inputs may be any that keep to these rules, and one draw needn't show every extreme that they name: `tile_place`: within one device's 24 slots the places are distinct. `tile_count`: some device uses all 24 slots in every draw.
All inputs are finite; a program needn't handle non-finite values.
Results may differ from the reference program's by a relative error of at most 0.002.
Values may be sent and summed in bfloat16 or wider, within the bound.
A program may use at most 128 MiB of HBM per device.

```python
import math
import jax
import jax.numpy as jnp
from jax import lax

K = 256
F = 4096
TILE = 128
USER_DEV = 1024
SHARDS = 32
PANEL = 32
ITEMS = 512
USERS = 32768
MAXT = 24
ALL_TILES = 768
N_MEM = 16


def draw_tile_place(key, part):
    key = jax.random.fold_in(key, 11)
    positions = USER_DEV // TILE * (ITEMS // TILE)
    subkeys = jax.random.split(key, SHARDS)
    chosen = jax.vmap(lambda subkey: jax.random.permutation(subkey, positions)[:MAXT])(subkeys)
    return chosen.reshape(SHARDS * MAXT).astype(jnp.int32)


def draw_tile_count(key, part):
    key = jax.random.fold_in(key, 23)
    first, second, third = jax.random.split(key, 3)
    lowest = max(1, MAXT // 8)
    highest = max(MAXT // 2, lowest) + 1
    counts = jax.random.randint(first, (SHARDS,), lowest, highest)
    busy = jax.random.randint(second, (SHARDS,), 0, 8) == 0
    counts = jnp.where(busy, MAXT, counts)
    forced = jax.random.randint(third, (), 0, SHARDS)
    counts = counts.at[forced].set(MAXT)
    return counts.astype(jnp.int32)


def with_spikes(array, rng, source, target, shards_of, factor):
    def block_of(position):
        return (jnp.arange(array.shape[position]) // (array.shape[position] // shards_of)).reshape((-1,) + (1,) * (array.ndim - 1 - position))

    near = jax.random.permutation(rng, shards_of)[block_of(target)]
    far = (block_of(target) + shards_of // 2) % shards_of
    return jnp.where((block_of(source) == near) | (block_of(source) == far), factor * array, array)


def level_of(rng, shape, pieces, least, top_value):
    loudness = 1.0
    for axis_at, blocks in pieces:
        draws = jax.random.uniform(jax.random.fold_in(jax.random.fold_in(rng, 6), axis_at), (blocks,), jnp.float32, least / len(pieces), top_value / len(pieces))
        loudness = loudness * jnp.repeat(jnp.exp(draws), shape[axis_at] // blocks).reshape((-1,) + (1,) * (len(shape) - 1 - axis_at))
    return loudness


def normal_values(key, shape, scale, bound, cuts=(), kind=jnp.bfloat16):
    values = scale * jax.random.normal(key, shape, jnp.float32)
    if cuts:
        values = values * level_of(key, shape, cuts, -0.22, 0.18)
    return jnp.clip(values, -bound, bound).astype(kind)


def heavy_noise(key, shape, spread, limit, shards, heavy, held_as=jnp.bfloat16):
    array = spread * jax.random.normal(key, shape, jnp.float32)
    if shards:
        array = array * level_of(key, shape, shards, -0.22, 0.18)
    return jnp.clip(with_spikes(array, jax.random.fold_in(key, 3), *heavy), -limit, limit).astype(held_as)


def setup_inputs(seed: int = 0) -> dict:
    streams_of = jax.random.split(jax.random.key(seed), 12)
    user_factors = normal_values(streams_of[0], (USERS, K), 0.25, 1.5, ((0, 32),))
    item_factors = normal_values(streams_of[1], (ITEMS, K), 0.25, 1.5, ((0, 16),))
    link_weights = normal_values(streams_of[2], (F, K), F ** -0.5, 0.09375)
    item_feat = heavy_noise(streams_of[3], (N_MEM, PANEL, F), 1.0, 6.0, ((0, 16), (1, 2)), (1, 2, 2, 2.0))
    tile_values = normal_values(streams_of[4], (ALL_TILES, TILE, TILE), 1.0, 6.0, ((0, 32),))
    tile_scale = jnp.clip(jnp.exp(math.log(2.0) - 2.0794415 * jax.random.uniform(streams_of[5], (ALL_TILES,), jnp.float32) ** level_of(streams_of[5], (ALL_TILES,), ((0, 32),), -0.2, 0.2)), 0.25, 2.0)
    tile_place = draw_tile_place(jax.random.fold_in(streams_of[11], 71), 0)
    tile_count = draw_tile_count(jax.random.fold_in(streams_of[11], 71), 0)
    user_noise = normal_values(streams_of[8], (USERS, K), 1.0, 6.0, ((0, 32),))
    item_noise = normal_values(streams_of[9], (N_MEM, PANEL, K), 1.0, 6.0, ((0, 16), (1, 2)))
    link_noise = normal_values(streams_of[10], (F, K), 1.0, 6.0, ((0, 32),))
    return {"user_factors": user_factors, "item_factors": item_factors, "link_weights": link_weights, "item_feat": item_feat, "tile_values": tile_values, "tile_scale": tile_scale, "tile_place": tile_place, "tile_count": tile_count, "user_noise": user_noise, "item_noise": item_noise, "link_noise": link_noise}


rate_user = 0.004
prior_user = 0.5
rate_item = 0.002
prior_item = 0.2
rate_link = 0.002
prior_link = 0.5
noise_scale = 0.1


def device_terms(users_dev, items_all, values, scales, places, live_count):
    user_tiles = USER_DEV // TILE
    item_tiles = ITEMS // TILE
    tile_rows = places // item_tiles
    tile_cols = places % item_tiles
    valid = jnp.arange(MAXT, dtype=jnp.int32) < live_count
    user_blocks = users_dev.reshape(user_tiles, TILE, K).astype(jnp.float32)
    item_blocks = items_all.reshape(item_tiles, TILE, K).astype(jnp.float32)
    picked_users = user_blocks[tile_rows]
    picked_items = item_blocks[tile_cols]
    predicted = jnp.einsum('tak,tbk->tab', picked_users, picked_items)
    rating = scales[:, None, None] * values.astype(jnp.float32)
    errors = jnp.where(valid[:, None, None], rating - predicted, 0.0).astype(jnp.bfloat16).astype(jnp.float32)
    user_terms = jnp.einsum('tab,tbk->tak', errors, picked_items)
    item_terms = jnp.einsum('tab,tak->tbk', errors, picked_users)
    user_grad = jax.ops.segment_sum(user_terms, tile_rows, user_tiles)
    item_grad = jax.ops.segment_sum(item_terms, tile_cols, item_tiles)
    return user_grad.reshape(USER_DEV, K), item_grad.reshape(ITEMS, K)


def reference(user_factors, item_factors, link_weights, item_feat, tile_values, tile_scale, tile_place, tile_count, user_noise, item_noise, link_noise):
    users_all = user_factors.reshape(SHARDS, USER_DEV, K)
    values_all = tile_values.reshape(SHARDS, MAXT, TILE, TILE)
    scales_all = tile_scale.reshape(SHARDS, MAXT)
    places_all = tile_place.reshape(SHARDS, MAXT)

    def advance(totals, inputs):
        users_dev, values, scales, places, live_count = inputs
        user_grad, item_grad = device_terms(users_dev, item_factors, values, scales, places, live_count)
        return totals + item_grad, user_grad

    item_total, user_grads = lax.scan(advance, jnp.zeros((ITEMS, K), jnp.float32),
                                      (users_all, values_all, scales_all, places_all, tile_count))
    user_grad = user_grads.reshape(USERS, K)
    old_users = user_factors.astype(jnp.float32)
    new_users = old_users + rate_user * user_grad - prior_user * old_users + noise_scale * user_noise.astype(jnp.float32)
    old_items = item_factors.reshape(N_MEM, PANEL, K).astype(jnp.float32)
    feats = item_feat.astype(jnp.float32)
    prior_mean = jnp.einsum('mpf,fk->mpk', feats, link_weights.astype(jnp.float32))
    resid = old_items - prior_mean
    resid_low = resid.astype(jnp.bfloat16).astype(jnp.float32)
    link_grad = jnp.einsum('mpf,mpk->fk', feats, resid_low)
    old_link = link_weights.astype(jnp.float32)
    new_link = old_link + rate_link * link_grad - prior_link * old_link + noise_scale * link_noise.astype(jnp.float32)
    item_grad = item_total.reshape(N_MEM, PANEL, K)
    new_items = old_items + rate_item * item_grad - prior_item * resid + noise_scale * item_noise.astype(jnp.float32)
    return new_users, new_items, new_link
```

```python
import functools

import jax
import jax.numpy as jnp
from jax import lax
from jax.experimental import pallas as pl
from jax.experimental.pallas import tpu as pltpu
from jax.sharding import PartitionSpec as P

rate_user = 0.004
prior_user = 0.5
rate_item = 0.002
prior_item = 0.2
rate_link = 0.002
prior_link = 0.5
noise_scale = 0.1

f32 = jnp.float32
bf16 = jnp.bfloat16
MESH = pl.DeviceIdType.MESH


def kernel(
    groups,
    members,
    slot_of,
    scales,
    panel,
    feats,
    cut,
    item_noise,
    link_noise,
    users_hbm,
    weights_hbm,
    tiles_hbm,
    noise_hbm,
    new_users,
    new_items,
    new_link,
    users,
    weights,
    tiles,
    noise,
    items,
    feat_all,
    resid_all,
    grad_send,
    grad_all,
    errors,
    user_sum,
    local_sem,
    send_sem,
    recv_sem,
):
    n = groups * members
    grp = lax.axis_index("grp")
    mem = lax.axis_index("mem")
    me = grp * members + mem
    own = mem * groups + grp
    panel_rows, rank = panel.shape
    owned = feats.shape[0]
    link_rows = link_noise.shape[0]
    side = tiles.shape[1]
    user_tiles = users.shape[0] // side
    item_tiles = items.shape[0] * panel_rows // side

    loads = [
        pltpu.make_async_copy(weights_hbm, weights, local_sem.at[0]),
        pltpu.make_async_copy(users_hbm, users, local_sem.at[1]),
        pltpu.make_async_copy(tiles_hbm, tiles, local_sem.at[2]),
        pltpu.make_async_copy(noise_hbm, noise, local_sem.at[3]),
    ]
    for load in loads:
        load.start()

    def place(d):
        return {"grp": d // members, "mem": lax.rem(d, members)}

    barrier = pltpu.get_barrier_semaphore()

    def greet(k, carry):
        d = lax.rem(me + k, n)
        pl.semaphore_signal(barrier, inc=1, device_id=place(d), device_id_type=MESH)
        return carry

    lax.fori_loop(1, n, greet, 0)
    items[mem] = panel[...]
    if cut is None:
        feat_all[me] = feats[:, pl.ds(pl.multiple_of(me * link_rows, link_rows), link_rows)]
    else:
        feat_all[me] = cut[me]
    pl.semaphore_wait(barrier, n - 1)

    def send_panel(k, carry):
        m = lax.rem(mem + k, members)
        pltpu.make_async_remote_copy(
            src_ref=panel,
            dst_ref=items.at[mem],
            send_sem=send_sem.at[0],
            recv_sem=recv_sem.at[0],
            device_id={"grp": grp, "mem": m},
            device_id_type=MESH,
        ).start()
        return carry

    lax.fori_loop(1, members, send_panel, 0)

    def send_feat(k, carry):
        d = lax.rem(me + k, n)
        if cut is None:
            source = feats.at[:, pl.ds(pl.multiple_of(d * link_rows, link_rows), link_rows)]
        else:
            source = cut.at[d]
        pltpu.make_async_remote_copy(
            src_ref=source,
            dst_ref=feat_all.at[me],
            send_sem=send_sem.at[1],
            recv_sem=recv_sem.at[1],
            device_id=place(d),
            device_id_type=MESH,
        ).start()
        return carry

    lax.fori_loop(1, n, send_feat, 0)

    loads[0].wait()
    start = pl.multiple_of(grp * owned, owned)
    own_items = panel[pl.ds(start, owned), :].astype(f32)
    resid = own_items - jnp.dot(feats[...], weights[...], preferred_element_type=f32)
    resid_all[me] = resid.astype(bf16)

    def send_resid(k, carry):
        d = lax.rem(me + k, n)
        pltpu.make_async_remote_copy(
            src_ref=resid_all.at[me],
            dst_ref=resid_all.at[me],
            send_sem=send_sem.at[2],
            recv_sem=recv_sem.at[2],
            device_id=place(d),
            device_id_type=MESH,
        ).start()
        return carry

    lax.fori_loop(1, n, send_resid, 0)

    def wait_all(buffer, count, sem):
        part = buffer.at[pl.ds(0, count)]
        pltpu.make_async_copy(part, part, sem).wait()

    loads[1].wait()
    loads[2].wait()
    wait_all(items, members - 1, recv_sem.at[0])

    wide = 2 if item_tiles % 2 == 0 else 1
    tall = 2 if user_tiles % 2 == 0 else 1
    chunk = wide * side
    panels_in = chunk // panel_rows
    owners_in = chunk // owned

    def do_chunk(c, first):
        block = items[pl.ds(c * panels_in, panels_in)].reshape(chunk, rank)
        for t in range(user_tiles // tall):
            rows = pl.ds(t * tall * side, tall * side)
            predicted = lax.dot_general(
                users[rows, :], block, (((1,), (1,)), ((), ())), preferred_element_type=f32
            )
            for a in range(tall):
                for b in range(wide):
                    slot = slot_of[(t * tall + a) * item_tiles + c * wide + b]
                    at = jnp.maximum(slot, 0)
                    live = (slot >= 0).astype(f32)
                    rating = scales[at] * tiles[at].astype(f32)
                    part = predicted[a * side : (a + 1) * side, b * side : (b + 1) * side]
                    errors[pl.ds((t * tall + a) * side, side), b * side : (b + 1) * side] = (
                        (rating - part) * live
                    ).astype(bf16)
            term = jnp.dot(errors[rows, :], block, preferred_element_type=f32)
            if first:
                user_sum[rows, :] = term
            else:
                user_sum[rows, :] += term
        grads = lax.dot_general(
            errors[...], users[...], (((0,), (0,)), ((), ())), preferred_element_type=f32
        )
        grad_send[pl.ds(c * owners_in, owners_in)] = grads.astype(bf16).reshape(
            owners_in, owned, rank
        )

        def send_grad(j, carry):
            o = c * owners_in + j

            @pl.when(o != own)
            def _():
                pltpu.make_async_remote_copy(
                    src_ref=grad_send.at[o],
                    dst_ref=grad_all.at[me],
                    send_sem=send_sem.at[3],
                    recv_sem=recv_sem.at[3],
                    device_id={"grp": lax.rem(o, groups), "mem": o // groups},
                    device_id_type=MESH,
                ).start()

            return carry

        lax.fori_loop(0, owners_in, send_grad, 0)

    chunks = item_tiles // wide
    if chunks <= 4:
        for c in range(chunks):
            do_chunk(c, c == 0)
    else:
        do_chunk(0, True)

        def later(c, carry):
            do_chunk(c, False)
            return carry

        lax.fori_loop(1, chunks, later, 0)

    loads[3].wait()
    for t in range(user_tiles):
        rows = pl.ds(t * side, side)
        user_sum[rows, :] = (
            (1.0 - prior_user) * users[rows, :].astype(f32)
            + rate_user * user_sum[rows, :]
            + noise_scale * noise[rows, :].astype(f32)
        )
    store = pltpu.make_async_copy(user_sum, new_users, local_sem.at[4])
    store.start()

    wait_all(feat_all, n - 1, recv_sem.at[1])
    wait_all(resid_all, n - 1, recv_sem.at[2])
    link_sum = lax.dot_general(
        feat_all[...].reshape(n * owned, link_rows),
        resid_all[...].reshape(n * owned, rank),
        (((0,), (0,)), ((), ())),
        preferred_element_type=f32,
    )
    old_link = weights[pl.ds(pl.multiple_of(me * link_rows, link_rows), link_rows), :].astype(f32)
    new_link[...] = (
        (1.0 - prior_link) * old_link
        + rate_link * link_sum
        + noise_scale * link_noise[...].astype(f32)
    )

    grad_all[me] = grad_send[own]
    wait_all(grad_all, n - 1, recv_sem.at[3])

    def gather(k, total):
        return total + jnp.sum(grad_all[pl.ds(k * 8, 8)].astype(f32), axis=0)

    item_sum = lax.fori_loop(0, n // 8, gather, jnp.zeros((owned, rank), f32))
    new_items[...] = (
        own_items
        + rate_item * item_sum
        - prior_item * resid
        + noise_scale * item_noise[...].astype(f32)
    )

    wait_all(items, members - 1, send_sem.at[0])
    wait_all(feat_all, n - 1, send_sem.at[1])
    wait_all(resid_all, n - 1, send_sem.at[2])
    wait_all(grad_all, n - 1, send_sem.at[3])
    store.wait()


def narrow_kernel(groups, members, *refs):
    kernel(groups, members, *refs[:4], None, *refs[4:])


def per_device(
    user_factors,
    item_factors,
    link_weights,
    item_feat,
    tile_values,
    tile_scale,
    tile_place,
    tile_count,
    user_noise,
    item_noise,
    link_noise,
):
    groups = lax.axis_size("grp")
    members = lax.axis_size("mem")
    n = groups * members
    slots, side, unused = tile_values.shape
    user_count, rank = user_factors.shape
    panel_rows = item_factors.shape[0]
    owned = item_feat.shape[1]
    features = item_feat.shape[2]
    link_rows = link_noise.shape[0]
    places = (user_count // side) * (panel_rows * members // side)
    numbers = jnp.arange(slots, dtype=jnp.int32)
    match = (tile_place[None, :] == jnp.arange(places, dtype=jnp.int32)[:, None]) & (
        numbers < tile_count[0]
    )[None, :]
    slot_of = jnp.max(jnp.where(match, numbers[None, :], -1), axis=1)
    feats = item_feat[0]

    smem = pl.BlockSpec(memory_space=pltpu.SMEM)
    vmem = pl.BlockSpec(memory_space=pltpu.VMEM)
    hbm = pl.BlockSpec(memory_space=pl.ANY)
    operands = [slot_of, tile_scale, item_factors, feats]
    specs = [smem, smem, vmem, vmem]
    if link_rows % 128:
        operands.append(feats.reshape(owned, n, link_rows).transpose(1, 0, 2))
        specs.append(vmem)
        body = functools.partial(kernel, groups, members)
    else:
        body = functools.partial(narrow_kernel, groups, members)
    operands += [item_noise[0], link_noise, user_factors, link_weights, tile_values, user_noise]
    specs += [vmem, vmem, hbm, hbm, hbm, hbm]
    chunk = 2 * side if (panel_rows * members // side) % 2 == 0 else side
    new_users, new_items, new_link = pl.pallas_call(
        body,
        out_shape=(
            jax.ShapeDtypeStruct((user_count, rank), f32),
            jax.ShapeDtypeStruct((owned, rank), f32),
            jax.ShapeDtypeStruct((link_rows, rank), f32),
        ),
        in_specs=specs,
        out_specs=(hbm, vmem, vmem),
        scratch_shapes=[
            pltpu.VMEM((user_count, rank), bf16),
            pltpu.VMEM((features, rank), bf16),
            pltpu.VMEM((slots, side, side), bf16),
            pltpu.VMEM((user_count, rank), bf16),
            pltpu.VMEM((members, panel_rows, rank), bf16),
            pltpu.VMEM((n, owned, link_rows), bf16),
            pltpu.VMEM((n, owned, rank), bf16),
            pltpu.VMEM((n, owned, rank), bf16),
            pltpu.VMEM((n, owned, rank), bf16),
            pltpu.VMEM((user_count, chunk), bf16),
            pltpu.VMEM((user_count, rank), f32),
            pltpu.SemaphoreType.DMA((5,)),
            pltpu.SemaphoreType.DMA((4,)),
            pltpu.SemaphoreType.DMA((4,)),
        ],
        compiler_params=pltpu.CompilerParams(
            collective_id=0, has_side_effects=True, vmem_limit_bytes=48 * 1024 * 1024
        ),
    )(*operands)
    return (new_users, new_items[None], new_link)


def solution(mesh):
    in_specs = (
        P(("grp", "mem"), None),
        P("mem", None),
        P(),
        P("mem", "grp", None),
        P(("grp", "mem"), None, None),
        P(("grp", "mem")),
        P(("grp", "mem")),
        P(("grp", "mem")),
        P(("grp", "mem"), None),
        P("mem", "grp", None),
        P(("grp", "mem"), None),
    )
    out_specs = (P(("grp", "mem"), None), P("mem", "grp", None), P(("grp", "mem"), None))
    return jax.shard_map(
        per_device, mesh=mesh, in_specs=in_specs, out_specs=out_specs, check_vma=False
    )
```

```python
import functools

import jax
import jax.numpy as jnp
from jax import lax
from jax.experimental import pallas as pl
from jax.experimental.pallas import tpu as pltpu
from jax.sharding import PartitionSpec as P

rate_user = 0.004
prior_user = 0.5
rate_item = 0.002
prior_item = 0.2
rate_link = 0.002
prior_link = 0.5
noise_scale = 0.1

f32 = jnp.float32
bf16 = jnp.bfloat16
MESH = pl.DeviceIdType.MESH
VMEM_BYTES = 60 * 1024 * 1024


def kernel(
    groups,
    members,
    wide_cut,
    slot_of,
    scales,
    panel_hbm,
    cut_hbm,
    item_noise_hbm,
    link_noise_hbm,
    feats_hbm,
    users_hbm,
    weights_hbm,
    tiles_hbm,
    noise_hbm,
    new_users,
    new_items,
    new_link,
    panel,
    cut,
    item_noise,
    link_noise,
    feats,
    users,
    weights,
    tiles,
    noise,
    items,
    feat_out,
    feat_pair,
    feat_all,
    resid_all,
    grad_part,
    grad_in,
    grad_send,
    grad_all,
    errors,
    user_sum,
    item_out,
    link_out,
    local_sem,
    send_sem,
    recv_sem,
    part_sem,
):
    n = groups * members
    ring = members // 2
    chips = n // 2
    grp = lax.axis_index("grp")
    mem = lax.axis_index("mem")
    core = lax.rem(mem, 2)
    other = 1 - core
    spot = mem // 2
    chip = grp * ring + spot
    me = grp * members + mem
    panel_rows, rank = panel.shape
    owned = feats.shape[0]
    link_rows = link_noise.shape[0]
    side = tiles.shape[1]
    user_tiles = users.shape[0] // side
    item_tiles = members * panel_rows // side
    sibling = {"grp": grp, "mem": spot * 2 + other}

    def load(source, target, k):
        return pltpu.make_async_copy(source, target, local_sem.at[k])

    loads = [
        load(panel_hbm, panel, 0),
        load(feats_hbm, feats, 1),
        load(weights_hbm, weights, 2),
        None if wide_cut else load(cut_hbm, cut, 3),
        load(users_hbm, users, 4),
        load(tiles_hbm, tiles, 5),
        load(noise_hbm, noise, 6),
        load(link_noise_hbm, link_noise, 7),
        load(item_noise_hbm, item_noise, 8),
    ]
    for one in loads:
        if one is not None:
            one.start()

    def mate(q):
        return {"grp": q // ring, "mem": lax.rem(q, ring) * 2 + core}

    def send(source, target, k, device):
        pltpu.make_async_remote_copy(
            src_ref=source,
            dst_ref=target,
            send_sem=send_sem.at[k],
            recv_sem=recv_sem.at[k],
            device_id=device,
            device_id_type=MESH,
        ).start()

    def wait_for(part, sem):
        pltpu.make_async_copy(part, part, sem).wait()

    barrier = pltpu.get_barrier_semaphore()
    pl.semaphore_signal(barrier, inc=1, device_id=sibling, device_id_type=MESH)

    def greet(k, carry):
        q = lax.rem(chip + k, chips)
        pl.semaphore_signal(barrier, inc=1, device_id=mate(q), device_id_type=MESH)
        return carry

    lax.fori_loop(1, chips, greet, 0)

    loads[0].wait()
    items[spot, core] = panel[...]
    loads[1].wait()
    if not wide_cut:
        loads[3].wait()

    def piece(d):
        if wide_cut:
            return feats[:, pl.ds(pl.multiple_of(d * link_rows, link_rows), link_rows)]
        return cut[d]

    def pack(q, carry):
        feat_pair[q, core] = piece(q * 2 + core)
        feat_out[q] = piece(q * 2 + other)
        return carry

    lax.fori_loop(0, chips, pack, 0)
    pl.semaphore_wait(barrier, chips)

    def send_panel(k, carry):
        q = lax.rem(spot + k, ring)
        send(panel, items.at[spot, core], 0, {"grp": grp, "mem": q * 2 + core})
        return carry

    lax.fori_loop(1, ring, send_panel, 0)
    send(feat_out, feat_pair.at[:, core], 1, sibling)

    loads[2].wait()
    start = pl.multiple_of(grp * owned, owned)
    own_items = panel[pl.ds(start, owned), :].astype(f32)
    resid = own_items - jnp.dot(feats[...], weights[...], preferred_element_type=f32)
    resid_all[chip, core] = resid.astype(bf16)

    def send_resid(k, carry):
        q = lax.rem(chip + k, chips)
        send(resid_all.at[chip, core], resid_all.at[chip, core], 2, mate(q))
        return carry

    lax.fori_loop(1, chips, send_resid, 0)

    wait_for(items.at[pl.ds(0, ring - 1), 0], recv_sem.at[0])
    send(items.at[:, core], items.at[:, core], 3, sibling)

    wait_for(feat_out, recv_sem.at[1])
    feat_all[chip] = feat_pair[chip]

    def send_feat(k, carry):
        q = lax.rem(chip + k, chips)
        send(feat_pair.at[q], feat_all.at[chip], 4, mate(q))
        return carry

    lax.fori_loop(1, chips, send_feat, 0)

    loads[4].wait()
    loads[5].wait()
    wait_for(items.at[:, other], recv_sem.at[3])

    wide = 2
    tall = 2 if user_tiles % 2 == 0 else 1
    chunk = wide * side
    spots_in = chunk // panel_rows // 2

    def do_chunk(c, first):
        block = items[pl.ds(c * spots_in, spots_in)].reshape(chunk, rank)
        for t in range(user_tiles // tall):
            rows = pl.ds(t * tall * side, tall * side)
            predicted = lax.dot_general(
                users[rows, :], block, (((1,), (1,)), ((), ())), preferred_element_type=f32
            )
            for a in range(tall):
                for b in range(wide):
                    slot = slot_of[(t * tall + a) * item_tiles + c * wide + b]
                    at = jnp.maximum(slot, 0)
                    live = (slot >= 0).astype(f32)
                    rating = scales[at] * tiles[at].astype(f32)
                    part = predicted[a * side : (a + 1) * side, b * side : (b + 1) * side]
                    errors[pl.ds((t * tall + a) * side, side), b * side : (b + 1) * side] = (
                        (rating - part) * live
                    ).astype(bf16)
            term = jnp.dot(errors[rows, :], block, preferred_element_type=f32)
            if first:
                user_sum[rows, :] = term
            else:
                user_sum[rows, :] += term
        grads = lax.dot_general(
            errors[...], users[...], (((0,), (0,)), ((), ())), preferred_element_type=f32
        )
        span = pl.ds(c * spots_in, spots_in)
        grad_part[span] = grads.reshape(spots_in, 2, groups, owned, rank)
        pltpu.make_async_remote_copy(
            src_ref=grad_part.at[span, other],
            dst_ref=grad_in.at[span],
            send_sem=send_sem.at[5],
            recv_sem=part_sem.at[c],
            device_id=sibling,
            device_id_type=MESH,
        ).start()

    def finish(c):
        span = pl.ds(c * spots_in, spots_in)
        wait_for(grad_in.at[span], part_sem.at[c])
        grad_send[span] = (grad_part[span, core] + grad_in[span]).astype(bf16)

        def send_grad(j, carry):
            at = lax.rem(j + chip, spots_in * groups)
            to = c * spots_in + at // groups
            g = lax.rem(at, groups)

            @pl.when(g * ring + to != chip)
            def _():
                send(
                    grad_send.at[to, g],
                    grad_all.at[chip],
                    6,
                    {"grp": g, "mem": to * 2 + core},
                )

            return carry

        lax.fori_loop(0, spots_in * groups, send_grad, 0)

    chunks = item_tiles // wide
    do_chunk(0, True)
    wait_for(resid_all.at[pl.ds(0, chips - 1), 0], recv_sem.at[2])
    send(resid_all.at[:, core], resid_all.at[:, core], 7, sibling)
    if chunks <= 4:
        for c in range(1, chunks):
            do_chunk(c, False)
            finish(c - 1)
    else:

        def later(c, carry):
            do_chunk(c, False)
            finish(c - 1)
            return carry

        lax.fori_loop(1, chunks, later, 0)
    finish(chunks - 1)

    loads[6].wait()
    for t in range(user_tiles):
        rows = pl.ds(t * side, side)
        user_sum[rows, :] = (
            (1.0 - prior_user) * users[rows, :].astype(f32)
            + rate_user * user_sum[rows, :]
            + noise_scale * noise[rows, :].astype(f32)
        )
    stores = [load(user_sum, new_users, 9)]
    stores[0].start()

    loads[7].wait()
    wait_for(feat_all.at[pl.ds(0, chips - 1)], recv_sem.at[4])
    wait_for(resid_all.at[:, other], recv_sem.at[7])
    link_sum = lax.dot_general(
        feat_all[...].reshape(n * owned, link_rows),
        resid_all[...].reshape(n * owned, rank),
        (((0,), (0,)), ((), ())),
        preferred_element_type=f32,
    )
    old_link = weights[pl.ds(pl.multiple_of(me * link_rows, link_rows), link_rows), :].astype(f32)
    link_out[...] = (
        (1.0 - prior_link) * old_link
        + rate_link * link_sum
        + noise_scale * link_noise[...].astype(f32)
    )
    stores.append(load(link_out, new_link, 10))
    stores[1].start()

    loads[8].wait()
    grad_all[chip] = grad_send[spot, grp]
    wait_for(grad_all.at[pl.ds(0, chips - 1)], recv_sem.at[6])

    def gather(k, total):
        return total + jnp.sum(grad_all[pl.ds(k * 8, 8)].astype(f32), axis=0)

    item_sum = lax.fori_loop(0, chips // 8, gather, jnp.zeros((owned, rank), f32))
    item_out[...] = (
        own_items
        + rate_item * item_sum
        - prior_item * resid
        + noise_scale * item_noise[...].astype(f32)
    )
    stores.append(load(item_out, new_items, 11))
    stores[2].start()

    wait_for(items.at[pl.ds(0, ring - 1), 0], send_sem.at[0])
    wait_for(feat_out, send_sem.at[1])
    wait_for(resid_all.at[pl.ds(0, chips - 1), 0], send_sem.at[2])
    wait_for(items.at[:, 0], send_sem.at[3])
    wait_for(feat_all.at[pl.ds(0, chips - 1)], send_sem.at[4])
    wait_for(grad_in, send_sem.at[5])
    wait_for(grad_all.at[pl.ds(0, chips - 1)], send_sem.at[6])
    wait_for(resid_all.at[:, 0], send_sem.at[7])
    for one in stores:
        one.wait()


def place_kernel(a, b, c, x, y, z, sem):
    copies = [
        pltpu.make_async_copy(source, target, sem.at[k])
        for k, (source, target) in enumerate(((a, x), (b, y), (c, z)))
    ]
    for copy in copies:
        copy.start()
    for copy in copies:
        copy.wait()


def per_device(
    user_factors,
    item_factors,
    link_weights,
    item_feat,
    tile_values,
    tile_scale,
    tile_place,
    tile_count,
    user_noise,
    item_noise,
    link_noise,
):
    groups = lax.axis_size("grp")
    members = lax.axis_size("mem")
    n = groups * members
    slots, side, unused = tile_values.shape
    user_count, rank = user_factors.shape
    panel_rows = item_factors.shape[0]
    owned = item_feat.shape[1]
    features = item_feat.shape[2]
    link_rows = link_noise.shape[0]
    places = (user_count // side) * (panel_rows * members // side)
    numbers = jnp.arange(slots, dtype=jnp.int32)
    match = (tile_place[None, :] == jnp.arange(places, dtype=jnp.int32)[:, None]) & (
        numbers < tile_count[0]
    )[None, :]
    slot_of = jnp.max(jnp.where(match, numbers[None, :], -1), axis=1)
    feats = item_feat[0]

    smem = pl.BlockSpec(memory_space=pltpu.SMEM)
    hbm = pl.BlockSpec(memory_space=pl.ANY)
    wide_cut = link_rows % 128 == 0
    if wide_cut:
        cut = item_noise[0]
    else:
        cut = feats.reshape(owned, n, link_rows).transpose(1, 0, 2)
    operands = [
        slot_of,
        tile_scale,
        item_factors,
        cut,
        item_noise[0],
        link_noise,
        feats,
        user_factors,
        link_weights,
        tile_values,
        user_noise,
    ]
    ring = members // 2
    chips = n // 2
    item_tiles = panel_rows * members // side
    shapes = (
        jax.ShapeDtypeStruct((user_count, rank), f32),
        jax.ShapeDtypeStruct((owned, rank), f32),
        jax.ShapeDtypeStruct((link_rows, rank), f32),
    )
    outs = pl.pallas_call(
        functools.partial(kernel, groups, members, wide_cut),
        out_shape=shapes,
        in_specs=[smem, smem] + [hbm] * 9,
        out_specs=(hbm, hbm, hbm),
        scratch_shapes=[pltpu.VMEM(x.shape, bf16) for x in operands[2:]]
        + [
            pltpu.VMEM((ring, 2, panel_rows, rank), bf16),
            pltpu.VMEM((chips, owned, link_rows), bf16),
            pltpu.VMEM((chips, 2, owned, link_rows), bf16),
            pltpu.VMEM((chips, 2, owned, link_rows), bf16),
            pltpu.VMEM((chips, 2, owned, rank), bf16),
            pltpu.VMEM((ring, 2, groups, owned, rank), f32),
            pltpu.VMEM((ring, groups, owned, rank), f32),
            pltpu.VMEM((ring, groups, owned, rank), bf16),
            pltpu.VMEM((chips, owned, rank), bf16),
            pltpu.VMEM((user_count, 2 * side), bf16),
            pltpu.VMEM((user_count, rank), f32),
            pltpu.VMEM((owned, rank), f32),
            pltpu.VMEM((link_rows, rank), f32),
            pltpu.SemaphoreType.DMA((12,)),
            pltpu.SemaphoreType.DMA((8,)),
            pltpu.SemaphoreType.DMA((8,)),
            pltpu.SemaphoreType.DMA((item_tiles // 2,)),
        ],
        compiler_params=pltpu.CompilerParams(
            collective_id=0, has_side_effects=True, vmem_limit_bytes=VMEM_BYTES
        ),
    )(*operands)
    new_users, new_items, new_link = pl.pallas_call(
        place_kernel,
        out_shape=shapes,
        in_specs=[hbm] * 3,
        out_specs=(hbm, hbm, hbm),
        scratch_shapes=[pltpu.SemaphoreType.DMA((3,))],
        compiler_params=pltpu.CompilerParams(vmem_limit_bytes=VMEM_BYTES),
    )(*outs)
    return (new_users, new_items[None], new_link)


def solution(mesh):
    in_specs = (
        P(("grp", "mem"), None),
        P("mem", None),
        P(),
        P("mem", "grp", None),
        P(("grp", "mem"), None, None),
        P(("grp", "mem")),
        P(("grp", "mem")),
        P(("grp", "mem")),
        P(("grp", "mem"), None),
        P("mem", "grp", None),
        P(("grp", "mem"), None),
    )
    out_specs = (P(("grp", "mem"), None), P("mem", "grp", None), P(("grp", "mem"), None))
    return jax.shard_map(
        per_device, mesh=mesh, in_specs=in_specs, out_specs=out_specs, check_vma=False
    )
```

```python
import functools

import jax
import jax.numpy as jnp
from jax import lax
from jax.experimental import pallas as pl
from jax.experimental.pallas import tpu as pltpu
from jax.sharding import PartitionSpec as P

rate_user = 0.004
prior_user = 0.5
rate_item = 0.002
prior_item = 0.2
rate_link = 0.002
prior_link = 0.5
noise_scale = 0.1

f32 = jnp.float32
bf16 = jnp.bfloat16
MESH = pl.DeviceIdType.MESH
VMEM_BYTES = 60 * 1024 * 1024


def kernel(
    groups,
    members,
    wide_cut,
    slot_place,
    live_slots,
    scales,
    panel_hbm,
    cut_hbm,
    item_noise_hbm,
    link_noise_hbm,
    feats_hbm,
    users_hbm,
    weights_hbm,
    tiles_hbm,
    noise_hbm,
    new_users,
    new_items,
    new_link,
    panel,
    cut,
    item_noise,
    link_noise,
    feats,
    users,
    weights,
    tiles,
    noise,
    items,
    feat_out,
    feat_pair,
    feat_all,
    resid_all,
    grad_part,
    grad_in,
    grad_send,
    grad_all,
    errors,
    user_sum,
    item_out,
    link_out,
    slot_of,
    local_sem,
    send_sem,
    recv_sem,
    part_sem,
):
    n = groups * members
    ring = members // 2
    chips = n // 2
    grp = lax.axis_index("grp")
    mem = lax.axis_index("mem")
    core = lax.rem(mem, 2)
    other = 1 - core
    spot = mem // 2
    chip = grp * ring + spot
    me = grp * members + mem
    panel_rows, rank = panel.shape
    owned = feats.shape[0]
    link_rows = link_noise.shape[0]
    side = tiles.shape[1]
    user_tiles = users.shape[0] // side
    item_tiles = members * panel_rows // side
    sibling = {"grp": grp, "mem": spot * 2 + other}

    def load(source, target, k):
        return pltpu.make_async_copy(source, target, local_sem.at[k])

    loads = [
        load(panel_hbm, panel, 0),
        load(feats_hbm, feats, 1),
        load(weights_hbm, weights, 2),
        None if wide_cut else load(cut_hbm, cut, 3),
        load(users_hbm, users, 4),
        load(tiles_hbm, tiles, 5),
        load(noise_hbm, noise, 6),
        load(link_noise_hbm, link_noise, 7),
        load(item_noise_hbm, item_noise, 8),
    ]
    for one in loads:
        if one is not None:
            one.start()

    def mate(q):
        return {"grp": q // ring, "mem": lax.rem(q, ring) * 2 + core}

    def send(source, target, k, device):
        pltpu.make_async_remote_copy(
            src_ref=source,
            dst_ref=target,
            send_sem=send_sem.at[k],
            recv_sem=recv_sem.at[k],
            device_id=device,
            device_id_type=MESH,
        ).start()

    def wait_for(part, sem):
        pltpu.make_async_copy(part, part, sem).wait()

    barrier = pltpu.get_barrier_semaphore()
    pl.semaphore_signal(barrier, inc=1, device_id=sibling, device_id_type=MESH)

    def greet(k, carry):
        q = lax.rem(chip + k, chips)
        pl.semaphore_signal(barrier, inc=1, device_id=mate(q), device_id_type=MESH)
        return carry

    lax.fori_loop(1, chips, greet, 0)

    slots = tiles.shape[0]
    step = 8 if slots % 8 == 0 else 1
    live_count = live_slots[0]

    def find(q, carry):
        def look(k, best):
            for j in range(step):
                at = k * step + j
                best = jnp.where((slot_place[at] == q) & (at < live_count), at, best)
            return best

        best = jnp.int32(-1)
        if slots <= 32:
            for k in range(slots // step):
                best = look(k, best)
        else:
            best = lax.fori_loop(0, slots // step, look, best)
        slot_of[q] = best
        return carry

    lax.fori_loop(0, user_tiles * item_tiles, find, 0)

    loads[0].wait()
    items[spot, core] = panel[...]
    loads[1].wait()
    if not wide_cut:
        loads[3].wait()

    def piece(d):
        if wide_cut:
            return feats[:, pl.ds(pl.multiple_of(d * link_rows, link_rows), link_rows)]
        return cut[d]

    def pack(q, carry):
        feat_pair[q, core] = piece(q * 2 + core)
        feat_out[q] = piece(q * 2 + other)
        return carry

    lax.fori_loop(0, chips, pack, 0)
    pl.semaphore_wait(barrier, chips)

    def send_panel(k, carry):
        q = lax.rem(spot + k, ring)
        send(panel, items.at[spot, core], 0, {"grp": grp, "mem": q * 2 + core})
        return carry

    lax.fori_loop(1, ring, send_panel, 0)
    send(feat_out, feat_pair.at[:, core], 1, sibling)

    loads[2].wait()
    start = pl.multiple_of(grp * owned, owned)
    own_items = panel[pl.ds(start, owned), :].astype(f32)
    resid = own_items - jnp.dot(feats[...], weights[...], preferred_element_type=f32)
    resid_all[chip, core] = resid.astype(bf16)

    def send_resid(k, carry):
        q = lax.rem(chip + k, chips)
        send(resid_all.at[chip, core], resid_all.at[chip, core], 2, mate(q))
        return carry

    lax.fori_loop(1, chips, send_resid, 0)

    wait_for(items.at[pl.ds(0, ring - 1), 0], recv_sem.at[0])
    send(items.at[:, core], items.at[:, core], 3, sibling)

    wait_for(feat_out, recv_sem.at[1])
    feat_all[chip] = feat_pair[chip]

    def send_feat(k, carry):
        q = lax.rem(chip + k, chips)
        send(feat_pair.at[q], feat_all.at[chip], 4, mate(q))
        return carry

    lax.fori_loop(1, chips, send_feat, 0)

    loads[4].wait()
    loads[5].wait()
    wait_for(items.at[:, other], recv_sem.at[3])

    wide = 2
    tall = 2 if user_tiles % 2 == 0 else 1
    chunk = wide * side
    spots_in = chunk // panel_rows // 2

    def do_chunk(c, first):
        block = items[pl.ds(c * spots_in, spots_in)].reshape(chunk, rank)
        for t in range(user_tiles // tall):
            rows = pl.ds(t * tall * side, tall * side)
            predicted = lax.dot_general(
                users[rows, :], block, (((1,), (1,)), ((), ())), preferred_element_type=f32
            )
            for a in range(tall):
                for b in range(wide):
                    slot = slot_of[(t * tall + a) * item_tiles + c * wide + b]
                    at = jnp.maximum(slot, 0)
                    live = (slot >= 0).astype(f32)
                    rating = scales[at] * tiles[at].astype(f32)
                    part = predicted[a * side : (a + 1) * side, b * side : (b + 1) * side]
                    errors[pl.ds((t * tall + a) * side, side), b * side : (b + 1) * side] = (
                        (rating - part) * live
                    ).astype(bf16)
            term = jnp.dot(errors[rows, :], block, preferred_element_type=f32)
            if first:
                user_sum[rows, :] = term
            else:
                user_sum[rows, :] += term
        grads = lax.dot_general(
            errors[...], users[...], (((0,), (0,)), ((), ())), preferred_element_type=f32
        )
        span = pl.ds(c * spots_in, spots_in)
        grad_part[span] = grads.reshape(spots_in, 2, groups, owned, rank)
        pltpu.make_async_remote_copy(
            src_ref=grad_part.at[span, other],
            dst_ref=grad_in.at[span],
            send_sem=send_sem.at[5],
            recv_sem=part_sem.at[c],
            device_id=sibling,
            device_id_type=MESH,
        ).start()

    def finish(c):
        span = pl.ds(c * spots_in, spots_in)
        wait_for(grad_in.at[span], part_sem.at[c])
        grad_send[span] = (grad_part[span, core] + grad_in[span]).astype(bf16)

        def send_grad(j, carry):
            at = lax.rem(j + chip, spots_in * groups)
            to = c * spots_in + at // groups
            g = lax.rem(at, groups)

            @pl.when(g * ring + to != chip)
            def _():
                send(
                    grad_send.at[to, g],
                    grad_all.at[chip],
                    6,
                    {"grp": g, "mem": to * 2 + core},
                )

            return carry

        lax.fori_loop(0, spots_in * groups, send_grad, 0)

    chunks = item_tiles // wide
    do_chunk(0, True)
    wait_for(resid_all.at[pl.ds(0, chips - 1), 0], recv_sem.at[2])
    send(resid_all.at[:, core], resid_all.at[:, core], 7, sibling)
    if chunks <= 4:
        for c in range(1, chunks):
            do_chunk(c, False)
            finish(c - 1)
    else:

        def later(c, carry):
            do_chunk(c, False)
            finish(c - 1)
            return carry

        lax.fori_loop(1, chunks, later, 0)
    finish(chunks - 1)

    loads[6].wait()
    for t in range(user_tiles):
        rows = pl.ds(t * side, side)
        user_sum[rows, :] = (
            (1.0 - prior_user) * users[rows, :].astype(f32)
            + rate_user * user_sum[rows, :]
            + noise_scale * noise[rows, :].astype(f32)
        )
    stores = [load(user_sum, new_users, 9)]
    stores[0].start()

    loads[7].wait()
    wait_for(feat_all.at[pl.ds(0, chips - 1)], recv_sem.at[4])
    wait_for(resid_all.at[:, other], recv_sem.at[7])
    link_sum = lax.dot_general(
        feat_all[...].reshape(n * owned, link_rows),
        resid_all[...].reshape(n * owned, rank),
        (((0,), (0,)), ((), ())),
        preferred_element_type=f32,
    )
    old_link = weights[pl.ds(pl.multiple_of(me * link_rows, link_rows), link_rows), :].astype(f32)
    link_out[...] = (
        (1.0 - prior_link) * old_link
        + rate_link * link_sum
        + noise_scale * link_noise[...].astype(f32)
    )
    stores.append(load(link_out, new_link, 10))
    stores[1].start()

    loads[8].wait()
    grad_all[chip] = grad_send[spot, grp]
    wait_for(grad_all.at[pl.ds(0, chips - 1)], recv_sem.at[6])

    def gather(k, total):
        return total + jnp.sum(grad_all[pl.ds(k * 8, 8)].astype(f32), axis=0)

    item_sum = lax.fori_loop(0, chips // 8, gather, jnp.zeros((owned, rank), f32))
    item_out[...] = (
        own_items
        + rate_item * item_sum
        - prior_item * resid
        + noise_scale * item_noise[...].astype(f32)
    )
    stores.append(load(item_out, new_items, 11))
    stores[2].start()

    wait_for(items.at[pl.ds(0, ring - 1), 0], send_sem.at[0])
    wait_for(feat_out, send_sem.at[1])
    wait_for(resid_all.at[pl.ds(0, chips - 1), 0], send_sem.at[2])
    wait_for(items.at[:, 0], send_sem.at[3])
    wait_for(feat_all.at[pl.ds(0, chips - 1)], send_sem.at[4])
    wait_for(grad_in, send_sem.at[5])
    wait_for(grad_all.at[pl.ds(0, chips - 1)], send_sem.at[6])
    wait_for(resid_all.at[:, 0], send_sem.at[7])
    for one in stores:
        one.wait()


def place_kernel(a, b, c, x, y, z, held_a, held_b, held_c, in_sem, out_sem):
    pieces = 8
    rows = a.shape[0] // pieces
    paths = [(b, held_b, y), (c, held_c, z)]
    for k in range(pieces):
        part = pl.ds(k * rows, rows)
        paths.append((a.at[part], held_a.at[part], x.at[part]))
    ins = [
        pltpu.make_async_copy(source, held, in_sem.at[k])
        for k, (source, held, target) in enumerate(paths)
    ]
    outs = [
        pltpu.make_async_copy(held, target, out_sem.at[k])
        for k, (source, held, target) in enumerate(paths)
    ]
    for copy in ins:
        copy.start()
    for first, second in zip(ins, outs):
        first.wait()
        second.start()
    for copy in outs:
        copy.wait()


def per_device(
    user_factors,
    item_factors,
    link_weights,
    item_feat,
    tile_values,
    tile_scale,
    tile_place,
    tile_count,
    user_noise,
    item_noise,
    link_noise,
):
    groups = lax.axis_size("grp")
    members = lax.axis_size("mem")
    n = groups * members
    slots, side, unused = tile_values.shape
    user_count, rank = user_factors.shape
    panel_rows = item_factors.shape[0]
    owned = item_feat.shape[1]
    features = item_feat.shape[2]
    link_rows = link_noise.shape[0]
    places = (user_count // side) * (panel_rows * members // side)
    feats = item_feat[0]

    smem = pl.BlockSpec(memory_space=pltpu.SMEM)
    hbm = pl.BlockSpec(memory_space=pl.ANY)
    wide_cut = link_rows % 128 == 0
    if wide_cut:
        cut = item_noise[0]
    else:
        cut = feats.reshape(owned, n, link_rows).transpose(1, 0, 2)
    operands = [
        tile_place,
        tile_count,
        tile_scale,
        item_factors,
        cut,
        item_noise[0],
        link_noise,
        feats,
        user_factors,
        link_weights,
        tile_values,
        user_noise,
    ]
    ring = members // 2
    chips = n // 2
    item_tiles = panel_rows * members // side
    shapes = (
        jax.ShapeDtypeStruct((user_count, rank), f32),
        jax.ShapeDtypeStruct((owned, rank), f32),
        jax.ShapeDtypeStruct((link_rows, rank), f32),
    )
    outs = pl.pallas_call(
        functools.partial(kernel, groups, members, wide_cut),
        out_shape=shapes,
        in_specs=[smem, smem, smem] + [hbm] * 9,
        out_specs=(hbm, hbm, hbm),
        scratch_shapes=[pltpu.VMEM(x.shape, bf16) for x in operands[3:]]
        + [
            pltpu.VMEM((ring, 2, panel_rows, rank), bf16),
            pltpu.VMEM((chips, owned, link_rows), bf16),
            pltpu.VMEM((chips, 2, owned, link_rows), bf16),
            pltpu.VMEM((chips, 2, owned, link_rows), bf16),
            pltpu.VMEM((chips, 2, owned, rank), bf16),
            pltpu.VMEM((ring, 2, groups, owned, rank), f32),
            pltpu.VMEM((ring, groups, owned, rank), f32),
            pltpu.VMEM((ring, groups, owned, rank), bf16),
            pltpu.VMEM((chips, owned, rank), bf16),
            pltpu.VMEM((user_count, 2 * side), bf16),
            pltpu.VMEM((user_count, rank), f32),
            pltpu.VMEM((owned, rank), f32),
            pltpu.VMEM((link_rows, rank), f32),
            pltpu.SMEM((places,), jnp.int32),
            pltpu.SemaphoreType.DMA((12,)),
            pltpu.SemaphoreType.DMA((8,)),
            pltpu.SemaphoreType.DMA((8,)),
            pltpu.SemaphoreType.DMA((item_tiles // 2,)),
        ],
        compiler_params=pltpu.CompilerParams(
            collective_id=0, has_side_effects=True, vmem_limit_bytes=VMEM_BYTES
        ),
    )(*operands)
    new_users, new_items, new_link = pl.pallas_call(
        place_kernel,
        out_shape=shapes,
        in_specs=[hbm] * 3,
        out_specs=(hbm, hbm, hbm),
        scratch_shapes=[pltpu.VMEM(x.shape, f32) for x in shapes]
        + [pltpu.SemaphoreType.DMA((10,)), pltpu.SemaphoreType.DMA((10,))],
        compiler_params=pltpu.CompilerParams(vmem_limit_bytes=VMEM_BYTES),
    )(*outs)
    return (new_users, new_items[None], new_link)


def solution(mesh):
    in_specs = (
        P(("grp", "mem"), None),
        P("mem", None),
        P(),
        P("mem", "grp", None),
        P(("grp", "mem"), None, None),
        P(("grp", "mem")),
        P(("grp", "mem")),
        P(("grp", "mem")),
        P(("grp", "mem"), None),
        P("mem", "grp", None),
        P(("grp", "mem"), None),
    )
    out_specs = (P(("grp", "mem"), None), P("mem", "grp", None), P(("grp", "mem"), None))
    return jax.shard_map(
        per_device, mesh=mesh, in_specs=in_specs, out_specs=out_specs, check_vma=False
    )
```

```python
import functools

import jax
import jax.numpy as jnp
from jax import lax
from jax.experimental import pallas as pl
from jax.experimental.pallas import tpu as pltpu
from jax.sharding import PartitionSpec as P

rate_user = 0.004
prior_user = 0.5
rate_item = 0.002
prior_item = 0.2
rate_link = 0.002
prior_link = 0.5
noise_scale = 0.1

f32 = jnp.float32
bf16 = jnp.bfloat16
MESH = pl.DeviceIdType.MESH
VMEM_BYTES = 60 * 1024 * 1024


def kernel(
    groups,
    members,
    wide_cut,
    slot_place,
    live_slots,
    scales,
    panel_hbm,
    cut_hbm,
    item_noise_hbm,
    link_noise_hbm,
    feats_hbm,
    users_hbm,
    weights_hbm,
    tiles_hbm,
    noise_hbm,
    new_users,
    new_items,
    new_link,
    panel,
    cut,
    item_noise,
    link_noise,
    feats,
    users,
    weights,
    tiles,
    noise,
    items,
    feat_out,
    feat_pair,
    feat_all,
    resid_all,
    grad_part,
    grad_in,
    grad_send,
    grad_all,
    errors,
    user_sum,
    item_out,
    link_out,
    slot_of,
    local_sem,
    send_sem,
    recv_sem,
    part_sem,
):
    n = groups * members
    ring = members // 2
    chips = n // 2
    grp = lax.axis_index("grp")
    mem = lax.axis_index("mem")
    core = lax.rem(mem, 2)
    other = 1 - core
    spot = mem // 2
    chip = grp * ring + spot
    me = grp * members + mem
    panel_rows, rank = panel.shape
    owned = feats.shape[0]
    link_rows = link_noise.shape[0]
    side = tiles.shape[1]
    user_tiles = users.shape[0] // side
    item_tiles = members * panel_rows // side
    sibling = {"grp": grp, "mem": spot * 2 + other}

    def load(source, target, k):
        return pltpu.make_async_copy(source, target, local_sem.at[k])

    loads = [
        load(panel_hbm, panel, 0),
        load(feats_hbm, feats, 1),
        load(weights_hbm, weights, 2),
        None if wide_cut else load(cut_hbm, cut, 3),
        load(users_hbm, users, 4),
        load(tiles_hbm, tiles, 5),
        load(noise_hbm, noise, 6),
        load(link_noise_hbm, link_noise, 7),
        load(item_noise_hbm, item_noise, 8),
    ]
    for one in loads:
        if one is not None:
            one.start()

    def mate(q):
        return {"grp": q // ring, "mem": lax.rem(q, ring) * 2 + core}

    def send(source, target, k, device):
        pltpu.make_async_remote_copy(
            src_ref=source,
            dst_ref=target,
            send_sem=send_sem.at[k],
            recv_sem=recv_sem.at[k],
            device_id=device,
            device_id_type=MESH,
        ).start()

    def wait_for(part, sem):
        pltpu.make_async_copy(part, part, sem).wait()

    barrier = pltpu.get_barrier_semaphore()
    pl.semaphore_signal(barrier, inc=1, device_id=sibling, device_id_type=MESH)

    def greet(k, carry):
        q = lax.rem(chip + k, chips)
        pl.semaphore_signal(barrier, inc=1, device_id=mate(q), device_id_type=MESH)
        return carry

    lax.fori_loop(1, chips, greet, 0)

    slots = tiles.shape[0]
    step = 8 if slots % 8 == 0 else 1
    live_count = live_slots[0]

    def find(q, carry):
        def look(k, best):
            for j in range(step):
                at = k * step + j
                best = jnp.where((slot_place[at] == q) & (at < live_count), at, best)
            return best

        best = jnp.int32(-1)
        if slots <= 32:
            for k in range(slots // step):
                best = look(k, best)
        else:
            best = lax.fori_loop(0, slots // step, look, best)
        slot_of[q] = best
        return carry

    lax.fori_loop(0, user_tiles * item_tiles, find, 0)

    loads[0].wait()
    items[spot, core] = panel[...]
    loads[1].wait()
    if not wide_cut:
        loads[3].wait()

    def piece(d):
        if wide_cut:
            return feats[:, pl.ds(pl.multiple_of(d * link_rows, link_rows), link_rows)]
        return cut[d]

    def pack(q, carry):
        feat_pair[q, core] = piece(q * 2 + core)
        feat_out[q] = piece(q * 2 + other)
        return carry

    lax.fori_loop(0, chips, pack, 0)
    pl.semaphore_wait(barrier, chips)

    def send_panel(k, carry):
        q = lax.rem(spot + k, ring)
        send(panel, items.at[spot, core], 0, {"grp": grp, "mem": q * 2 + core})
        return carry

    lax.fori_loop(1, ring, send_panel, 0)
    send(feat_out, feat_pair.at[:, core], 1, sibling)

    loads[2].wait()
    start = pl.multiple_of(grp * owned, owned)
    own_items = panel[pl.ds(start, owned), :].astype(f32)
    resid = own_items - jnp.dot(feats[...], weights[...], preferred_element_type=f32)
    resid_all[chip, core] = resid.astype(bf16)

    def send_resid(k, carry):
        q = lax.rem(chip + k, chips)
        send(resid_all.at[chip, core], resid_all.at[chip, core], 2, mate(q))
        return carry

    lax.fori_loop(1, chips, send_resid, 0)

    wait_for(items.at[pl.ds(0, ring - 1), 0], recv_sem.at[0])
    send(items.at[:, core], items.at[:, core], 3, sibling)

    wait_for(feat_out, recv_sem.at[1])
    feat_all[chip] = feat_pair[chip]

    def send_feat(k, carry):
        q = lax.rem(chip + k, chips)
        send(feat_pair.at[q], feat_all.at[chip], 4, mate(q))
        return carry

    lax.fori_loop(1, chips, send_feat, 0)

    loads[4].wait()
    loads[5].wait()
    wait_for(items.at[:, other], recv_sem.at[3])

    wide = 2
    tall = 2 if user_tiles % 2 == 0 else 1
    chunk = wide * side
    spots_in = chunk // panel_rows // 2

    def do_chunk(c, first):
        block = items[pl.ds(c * spots_in, spots_in)].reshape(chunk, rank)
        for t in range(user_tiles // tall):
            rows = pl.ds(t * tall * side, tall * side)
            predicted = lax.dot_general(
                users[rows, :], block, (((1,), (1,)), ((), ())), preferred_element_type=f32
            )
            for a in range(tall):
                for b in range(wide):
                    slot = slot_of[(t * tall + a) * item_tiles + c * wide + b]
                    at = jnp.maximum(slot, 0)
                    live = (slot >= 0).astype(f32)
                    rating = scales[at] * tiles[at].astype(f32)
                    part = predicted[a * side : (a + 1) * side, b * side : (b + 1) * side]
                    errors[pl.ds((t * tall + a) * side, side), b * side : (b + 1) * side] = (
                        (rating - part) * live
                    ).astype(bf16)
            term = jnp.dot(errors[rows, :], block, preferred_element_type=f32)
            if first:
                user_sum[rows, :] = term
            else:
                user_sum[rows, :] += term
        grads = lax.dot_general(
            errors[...], users[...], (((0,), (0,)), ((), ())), preferred_element_type=f32
        )
        span = pl.ds(c * spots_in, spots_in)
        grad_part[span] = grads.reshape(spots_in, 2, groups, owned, rank)
        pltpu.make_async_remote_copy(
            src_ref=grad_part.at[span, other],
            dst_ref=grad_in.at[span],
            send_sem=send_sem.at[5],
            recv_sem=part_sem.at[c],
            device_id=sibling,
            device_id_type=MESH,
        ).start()

    def finish(c):
        span = pl.ds(c * spots_in, spots_in)
        wait_for(grad_in.at[span], part_sem.at[c])
        grad_send[span] = (grad_part[span, core] + grad_in[span]).astype(bf16)

        def send_grad(j, carry):
            at = lax.rem(j + chip, spots_in * groups)
            to = c * spots_in + at // groups
            g = lax.rem(at, groups)

            @pl.when(g * ring + to != chip)
            def _():
                send(
                    grad_send.at[to, g],
                    grad_all.at[chip],
                    6,
                    {"grp": g, "mem": to * 2 + core},
                )

            return carry

        lax.fori_loop(0, spots_in * groups, send_grad, 0)

    chunks = item_tiles // wide
    do_chunk(0, True)
    wait_for(resid_all.at[pl.ds(0, chips - 1), 0], recv_sem.at[2])
    send(resid_all.at[:, core], resid_all.at[:, core], 7, sibling)
    if chunks <= 4:
        for c in range(1, chunks):
            do_chunk(c, False)
            finish(c - 1)
    else:

        def later(c, carry):
            do_chunk(c, False)
            finish(c - 1)
            return carry

        lax.fori_loop(1, chunks, later, 0)

    loads[6].wait()
    for t in range(user_tiles):
        rows = pl.ds(t * side, side)
        user_sum[rows, :] = (
            (1.0 - prior_user) * users[rows, :].astype(f32)
            + rate_user * user_sum[rows, :]
            + noise_scale * noise[rows, :].astype(f32)
        )
    stores = [load(user_sum, new_users, 9)]
    stores[0].start()
    finish(chunks - 1)

    loads[7].wait()
    wait_for(feat_all.at[pl.ds(0, chips - 1)], recv_sem.at[4])
    wait_for(resid_all.at[:, other], recv_sem.at[7])
    link_sum = lax.dot_general(
        feat_all[...].reshape(n * owned, link_rows),
        resid_all[...].reshape(n * owned, rank),
        (((0,), (0,)), ((), ())),
        preferred_element_type=f32,
    )
    old_link = weights[pl.ds(pl.multiple_of(me * link_rows, link_rows), link_rows), :].astype(f32)
    link_out[...] = (
        (1.0 - prior_link) * old_link
        + rate_link * link_sum
        + noise_scale * link_noise[...].astype(f32)
    )
    stores.append(load(link_out, new_link, 10))
    stores[1].start()

    loads[8].wait()
    grad_all[chip] = grad_send[spot, grp]
    wait_for(grad_all.at[pl.ds(0, chips - 1)], recv_sem.at[6])

    def gather(k, total):
        return total + jnp.sum(grad_all[pl.ds(k * 8, 8)].astype(f32), axis=0)

    item_sum = lax.fori_loop(0, chips // 8, gather, jnp.zeros((owned, rank), f32))
    item_out[...] = (
        own_items
        + rate_item * item_sum
        - prior_item * resid
        + noise_scale * item_noise[...].astype(f32)
    )
    stores.append(load(item_out, new_items, 11))
    stores[2].start()

    wait_for(items.at[pl.ds(0, ring - 1), 0], send_sem.at[0])
    wait_for(feat_out, send_sem.at[1])
    wait_for(resid_all.at[pl.ds(0, chips - 1), 0], send_sem.at[2])
    wait_for(items.at[:, 0], send_sem.at[3])
    wait_for(feat_all.at[pl.ds(0, chips - 1)], send_sem.at[4])
    wait_for(grad_in, send_sem.at[5])
    wait_for(grad_all.at[pl.ds(0, chips - 1)], send_sem.at[6])
    wait_for(resid_all.at[:, 0], send_sem.at[7])
    for one in stores:
        one.wait()


def place_kernel(a, b, c, x, y, z, held_a, held_b, held_c, in_sem, out_sem):
    pieces = 8
    rows = a.shape[0] // pieces
    paths = [(b, held_b, y), (c, held_c, z)]
    for k in range(pieces):
        part = pl.ds(k * rows, rows)
        paths.append((a.at[part], held_a.at[part], x.at[part]))
    ins = [
        pltpu.make_async_copy(source, held, in_sem.at[k])
        for k, (source, held, target) in enumerate(paths)
    ]
    outs = [
        pltpu.make_async_copy(held, target, out_sem.at[k])
        for k, (source, held, target) in enumerate(paths)
    ]
    for copy in ins:
        copy.start()
    for first, second in zip(ins, outs):
        first.wait()
        second.start()
    for copy in outs:
        copy.wait()


def per_device(
    user_factors,
    item_factors,
    link_weights,
    item_feat,
    tile_values,
    tile_scale,
    tile_place,
    tile_count,
    user_noise,
    item_noise,
    link_noise,
):
    groups = lax.axis_size("grp")
    members = lax.axis_size("mem")
    n = groups * members
    slots, side, unused = tile_values.shape
    user_count, rank = user_factors.shape
    panel_rows = item_factors.shape[0]
    owned = item_feat.shape[1]
    features = item_feat.shape[2]
    link_rows = link_noise.shape[0]
    places = (user_count // side) * (panel_rows * members // side)
    feats = item_feat[0]

    smem = pl.BlockSpec(memory_space=pltpu.SMEM)
    hbm = pl.BlockSpec(memory_space=pl.ANY)
    wide_cut = link_rows % 128 == 0
    if wide_cut:
        cut = item_noise[0]
    else:
        cut = feats.reshape(owned, n, link_rows).transpose(1, 0, 2)
    operands = [
        tile_place,
        tile_count,
        tile_scale,
        item_factors,
        cut,
        item_noise[0],
        link_noise,
        feats,
        user_factors,
        link_weights,
        tile_values,
        user_noise,
    ]
    ring = members // 2
    chips = n // 2
    item_tiles = panel_rows * members // side
    shapes = (
        jax.ShapeDtypeStruct((user_count, rank), f32),
        jax.ShapeDtypeStruct((owned, rank), f32),
        jax.ShapeDtypeStruct((link_rows, rank), f32),
    )
    outs = pl.pallas_call(
        functools.partial(kernel, groups, members, wide_cut),
        out_shape=shapes,
        in_specs=[smem, smem, smem] + [hbm] * 9,
        out_specs=(hbm, hbm, hbm),
        scratch_shapes=[pltpu.VMEM(x.shape, bf16) for x in operands[3:]]
        + [
            pltpu.VMEM((ring, 2, panel_rows, rank), bf16),
            pltpu.VMEM((chips, owned, link_rows), bf16),
            pltpu.VMEM((chips, 2, owned, link_rows), bf16),
            pltpu.VMEM((chips, 2, owned, link_rows), bf16),
            pltpu.VMEM((chips, 2, owned, rank), bf16),
            pltpu.VMEM((ring, 2, groups, owned, rank), f32),
            pltpu.VMEM((ring, groups, owned, rank), f32),
            pltpu.VMEM((ring, groups, owned, rank), bf16),
            pltpu.VMEM((chips, owned, rank), bf16),
            pltpu.VMEM((user_count, 2 * side), bf16),
            pltpu.VMEM((user_count, rank), f32),
            pltpu.VMEM((owned, rank), f32),
            pltpu.VMEM((link_rows, rank), f32),
            pltpu.SMEM((places,), jnp.int32),
            pltpu.SemaphoreType.DMA((12,)),
            pltpu.SemaphoreType.DMA((8,)),
            pltpu.SemaphoreType.DMA((8,)),
            pltpu.SemaphoreType.DMA((item_tiles // 2,)),
        ],
        compiler_params=pltpu.CompilerParams(
            collective_id=0, has_side_effects=True, vmem_limit_bytes=VMEM_BYTES
        ),
    )(*operands)
    new_users, new_items, new_link = pl.pallas_call(
        place_kernel,
        out_shape=shapes,
        in_specs=[hbm] * 3,
        out_specs=(hbm, hbm, hbm),
        scratch_shapes=[pltpu.VMEM(x.shape, f32) for x in shapes]
        + [pltpu.SemaphoreType.DMA((10,)), pltpu.SemaphoreType.DMA((10,))],
        compiler_params=pltpu.CompilerParams(vmem_limit_bytes=VMEM_BYTES),
    )(*outs)
    return (new_users, new_items[None], new_link)


def solution(mesh):
    in_specs = (
        P(("grp", "mem"), None),
        P("mem", None),
        P(),
        P("mem", "grp", None),
        P(("grp", "mem"), None, None),
        P(("grp", "mem")),
        P(("grp", "mem")),
        P(("grp", "mem")),
        P(("grp", "mem"), None),
        P("mem", "grp", None),
        P(("grp", "mem"), None),
    )
    out_specs = (P(("grp", "mem"), None), P("mem", "grp", None), P(("grp", "mem"), None))
    return jax.shard_map(
        per_device, mesh=mesh, in_specs=in_specs, out_specs=out_specs, check_vma=False
    )
```

```python
import functools

import jax
import jax.numpy as jnp
from jax import lax
from jax.experimental import pallas as pl
from jax.experimental.pallas import tpu as pltpu
from jax.sharding import PartitionSpec as P

rate_user = 0.004
prior_user = 0.5
rate_item = 0.002
prior_item = 0.2
rate_link = 0.002
prior_link = 0.5
noise_scale = 0.1

f32 = jnp.float32
bf16 = jnp.bfloat16
MESH = pl.DeviceIdType.MESH
VMEM_BYTES = 60 * 1024 * 1024


def kernel(
    groups,
    members,
    wide_cut,
    slot_place,
    live_slots,
    scales,
    panel_hbm,
    cut_hbm,
    item_noise_hbm,
    link_noise_hbm,
    feats_hbm,
    users_hbm,
    weights_hbm,
    tiles_hbm,
    noise_hbm,
    new_users,
    new_items,
    new_link,
    panel,
    cut,
    item_noise,
    link_noise,
    feats,
    users,
    weights,
    tiles,
    noise,
    items,
    feat_out,
    feat_pair,
    feat_all,
    resid_all,
    grad_part,
    grad_in,
    grad_send,
    grad_all,
    errors,
    user_sum,
    item_out,
    link_out,
    slot_of,
    local_sem,
    send_sem,
    recv_sem,
    part_sem,
):
    n = groups * members
    ring = members // 2
    chips = n // 2
    grp = lax.axis_index("grp")
    mem = lax.axis_index("mem")
    core = lax.rem(mem, 2)
    other = 1 - core
    spot = mem // 2
    chip = grp * ring + spot
    me = grp * members + mem
    panel_rows, rank = panel.shape
    owned = feats.shape[0]
    link_rows = link_noise.shape[0]
    side = tiles.shape[1]
    user_tiles = users.shape[0] // side
    item_tiles = members * panel_rows // side
    sibling = {"grp": grp, "mem": spot * 2 + other}

    def load(source, target, k):
        return pltpu.make_async_copy(source, target, local_sem.at[k])

    loads = [
        load(panel_hbm, panel, 0),
        load(feats_hbm, feats, 1),
        load(weights_hbm, weights, 2),
        None if wide_cut else load(cut_hbm, cut, 3),
        load(users_hbm, users, 4),
        load(tiles_hbm, tiles, 5),
        load(noise_hbm, noise, 6),
        load(link_noise_hbm, link_noise, 7),
        load(item_noise_hbm, item_noise, 8),
    ]
    for one in loads:
        if one is not None:
            one.start()

    def mate(q):
        return {"grp": q // ring, "mem": lax.rem(q, ring) * 2 + core}

    def send(source, target, k, device):
        pltpu.make_async_remote_copy(
            src_ref=source,
            dst_ref=target,
            send_sem=send_sem.at[k],
            recv_sem=recv_sem.at[k],
            device_id=device,
            device_id_type=MESH,
        ).start()

    def wait_for(part, sem):
        pltpu.make_async_copy(part, part, sem).wait()

    barrier = pltpu.get_barrier_semaphore()
    pl.semaphore_signal(barrier, inc=1, device_id=sibling, device_id_type=MESH)

    def greet(k, carry):
        q = lax.rem(chip + k, chips)
        pl.semaphore_signal(barrier, inc=1, device_id=mate(q), device_id_type=MESH)
        return carry

    lax.fori_loop(1, chips, greet, 0)

    slots = tiles.shape[0]
    step = 8 if slots % 8 == 0 else 1
    live_count = live_slots[0]

    def find(q, carry):
        def look(k, best):
            for j in range(step):
                at = k * step + j
                best = jnp.where((slot_place[at] == q) & (at < live_count), at, best)
            return best

        best = jnp.int32(-1)
        if slots <= 32:
            for k in range(slots // step):
                best = look(k, best)
        else:
            best = lax.fori_loop(0, slots // step, look, best)
        slot_of[q] = best
        return carry

    lax.fori_loop(0, user_tiles * item_tiles, find, 0)

    loads[0].wait()
    items[spot, core] = panel[...]
    loads[1].wait()
    if not wide_cut:
        loads[3].wait()

    def piece(d):
        if wide_cut:
            return feats[:, pl.ds(pl.multiple_of(d * link_rows, link_rows), link_rows)]
        return cut[d]

    def pack(q, carry):
        feat_pair[q, core] = piece(q * 2 + core)
        feat_out[q] = piece(q * 2 + other)
        return carry

    lax.fori_loop(0, chips, pack, 0)
    pl.semaphore_wait(barrier, chips)

    def send_panel(k, carry):
        q = lax.rem(spot + k, ring)
        send(panel, items.at[spot, core], 0, {"grp": grp, "mem": q * 2 + core})
        return carry

    lax.fori_loop(1, ring, send_panel, 0)
    send(feat_out, feat_pair.at[:, core], 1, sibling)

    loads[2].wait()
    start = pl.multiple_of(grp * owned, owned)
    own_items = panel[pl.ds(start, owned), :].astype(f32)
    resid = own_items - jnp.dot(feats[...], weights[...], preferred_element_type=f32)
    resid_all[chip, core] = resid.astype(bf16)

    wait_for(items.at[pl.ds(0, ring - 1), 0], recv_sem.at[0])
    send(items.at[:, core], items.at[:, core], 3, sibling)

    def send_resid(k, carry):
        q = lax.rem(chip + k, chips)
        send(resid_all.at[chip, core], resid_all.at[chip, core], 2, mate(q))
        return carry

    lax.fori_loop(1, chips, send_resid, 0)

    wait_for(feat_out, recv_sem.at[1])
    feat_all[chip] = feat_pair[chip]

    def send_feat(k, carry):
        q = lax.rem(chip + k, chips)
        send(feat_pair.at[q], feat_all.at[chip], 4, mate(q))
        return carry

    lax.fori_loop(1, chips, send_feat, 0)

    loads[4].wait()
    loads[5].wait()
    wait_for(items.at[:, other], recv_sem.at[3])

    wide = 2
    tall = 2 if user_tiles % 2 == 0 else 1
    chunk = wide * side
    spots_in = chunk // panel_rows // 2

    def do_chunk(c, first):
        block = items[pl.ds(c * spots_in, spots_in)].reshape(chunk, rank)
        for t in range(user_tiles // tall):
            rows = pl.ds(t * tall * side, tall * side)
            predicted = lax.dot_general(
                users[rows, :], block, (((1,), (1,)), ((), ())), preferred_element_type=f32
            )
            for a in range(tall):
                for b in range(wide):
                    slot = slot_of[(t * tall + a) * item_tiles + c * wide + b]
                    at = jnp.maximum(slot, 0)
                    live = (slot >= 0).astype(f32)
                    rating = scales[at] * tiles[at].astype(f32)
                    part = predicted[a * side : (a + 1) * side, b * side : (b + 1) * side]
                    errors[pl.ds((t * tall + a) * side, side), b * side : (b + 1) * side] = (
                        (rating - part) * live
                    ).astype(bf16)
            term = jnp.dot(errors[rows, :], block, preferred_element_type=f32)
            if first:
                user_sum[rows, :] = term
            else:
                user_sum[rows, :] += term
        grads = lax.dot_general(
            errors[...], users[...], (((0,), (0,)), ((), ())), preferred_element_type=f32
        )
        span = pl.ds(c * spots_in, spots_in)
        grad_part[span] = grads.reshape(spots_in, 2, groups, owned, rank)
        pltpu.make_async_remote_copy(
            src_ref=grad_part.at[span, other],
            dst_ref=grad_in.at[span],
            send_sem=send_sem.at[5],
            recv_sem=part_sem.at[c],
            device_id=sibling,
            device_id_type=MESH,
        ).start()

    def finish(c):
        span = pl.ds(c * spots_in, spots_in)
        wait_for(grad_in.at[span], part_sem.at[c])
        grad_send[span] = (grad_part[span, core] + grad_in[span]).astype(bf16)

        def send_grad(j, carry):
            at = lax.rem(j + chip, spots_in * groups)
            to = c * spots_in + at // groups
            g = lax.rem(at, groups)

            @pl.when(g * ring + to != chip)
            def _():
                send(
                    grad_send.at[to, g],
                    grad_all.at[chip],
                    6,
                    {"grp": g, "mem": to * 2 + core},
                )

            return carry

        lax.fori_loop(0, spots_in * groups, send_grad, 0)

    chunks = item_tiles // wide
    do_chunk(0, True)
    wait_for(resid_all.at[pl.ds(0, chips - 1), 0], recv_sem.at[2])
    send(resid_all.at[:, core], resid_all.at[:, core], 7, sibling)
    if chunks <= 4:
        for c in range(1, chunks):
            do_chunk(c, False)
            finish(c - 1)
    else:

        def later(c, carry):
            do_chunk(c, False)
            finish(c - 1)
            return carry

        lax.fori_loop(1, chunks, later, 0)

    loads[6].wait()
    for t in range(user_tiles):
        rows = pl.ds(t * side, side)
        user_sum[rows, :] = (
            (1.0 - prior_user) * users[rows, :].astype(f32)
            + rate_user * user_sum[rows, :]
            + noise_scale * noise[rows, :].astype(f32)
        )
    stores = [load(user_sum, new_users, 9)]
    stores[0].start()
    finish(chunks - 1)

    loads[7].wait()
    wait_for(feat_all.at[pl.ds(0, chips - 1)], recv_sem.at[4])
    wait_for(resid_all.at[:, other], recv_sem.at[7])
    link_sum = lax.dot_general(
        feat_all[...].reshape(n * owned, link_rows),
        resid_all[...].reshape(n * owned, rank),
        (((0,), (0,)), ((), ())),
        preferred_element_type=f32,
    )
    old_link = weights[pl.ds(pl.multiple_of(me * link_rows, link_rows), link_rows), :].astype(f32)
    link_out[...] = (
        (1.0 - prior_link) * old_link
        + rate_link * link_sum
        + noise_scale * link_noise[...].astype(f32)
    )
    stores.append(load(link_out, new_link, 10))
    stores[1].start()

    loads[8].wait()
    grad_all[chip] = grad_send[spot, grp]
    wait_for(grad_all.at[pl.ds(0, chips - 1)], recv_sem.at[6])

    def gather(k, total):
        return total + jnp.sum(grad_all[pl.ds(k * 8, 8)].astype(f32), axis=0)

    item_sum = lax.fori_loop(0, chips // 8, gather, jnp.zeros((owned, rank), f32))
    item_out[...] = (
        own_items
        + rate_item * item_sum
        - prior_item * resid
        + noise_scale * item_noise[...].astype(f32)
    )
    stores.append(load(item_out, new_items, 11))
    stores[2].start()

    wait_for(items.at[pl.ds(0, ring - 1), 0], send_sem.at[0])
    wait_for(feat_out, send_sem.at[1])
    wait_for(resid_all.at[pl.ds(0, chips - 1), 0], send_sem.at[2])
    wait_for(items.at[:, 0], send_sem.at[3])
    wait_for(feat_all.at[pl.ds(0, chips - 1)], send_sem.at[4])
    wait_for(grad_in, send_sem.at[5])
    wait_for(grad_all.at[pl.ds(0, chips - 1)], send_sem.at[6])
    wait_for(resid_all.at[:, 0], send_sem.at[7])
    for one in stores:
        one.wait()


def place_kernel(a, b, c, x, y, z, held_a, held_b, held_c, in_sem, out_sem):
    pieces = 8
    rows = a.shape[0] // pieces
    paths = [(b, held_b, y), (c, held_c, z)]
    for k in range(pieces):
        part = pl.ds(k * rows, rows)
        paths.append((a.at[part], held_a.at[part], x.at[part]))
    ins = [
        pltpu.make_async_copy(source, held, in_sem.at[k])
        for k, (source, held, target) in enumerate(paths)
    ]
    outs = [
        pltpu.make_async_copy(held, target, out_sem.at[k])
        for k, (source, held, target) in enumerate(paths)
    ]
    for copy in ins:
        copy.start()
    for first, second in zip(ins, outs):
        first.wait()
        second.start()
    for copy in outs:
        copy.wait()


def per_device(
    user_factors,
    item_factors,
    link_weights,
    item_feat,
    tile_values,
    tile_scale,
    tile_place,
    tile_count,
    user_noise,
    item_noise,
    link_noise,
):
    groups = lax.axis_size("grp")
    members = lax.axis_size("mem")
    n = groups * members
    slots, side, unused = tile_values.shape
    user_count, rank = user_factors.shape
    panel_rows = item_factors.shape[0]
    owned = item_feat.shape[1]
    features = item_feat.shape[2]
    link_rows = link_noise.shape[0]
    places = (user_count // side) * (panel_rows * members // side)
    feats = item_feat[0]

    smem = pl.BlockSpec(memory_space=pltpu.SMEM)
    hbm = pl.BlockSpec(memory_space=pl.ANY)
    wide_cut = link_rows % 128 == 0
    if wide_cut:
        cut = item_noise[0]
    else:
        cut = feats.reshape(owned, n, link_rows).transpose(1, 0, 2)
    operands = [
        tile_place,
        tile_count,
        tile_scale,
        item_factors,
        cut,
        item_noise[0],
        link_noise,
        feats,
        user_factors,
        link_weights,
        tile_values,
        user_noise,
    ]
    ring = members // 2
    chips = n // 2
    item_tiles = panel_rows * members // side
    shapes = (
        jax.ShapeDtypeStruct((user_count, rank), f32),
        jax.ShapeDtypeStruct((owned, rank), f32),
        jax.ShapeDtypeStruct((link_rows, rank), f32),
    )
    outs = pl.pallas_call(
        functools.partial(kernel, groups, members, wide_cut),
        out_shape=shapes,
        in_specs=[smem, smem, smem] + [hbm] * 9,
        out_specs=(hbm, hbm, hbm),
        scratch_shapes=[pltpu.VMEM(x.shape, bf16) for x in operands[3:]]
        + [
            pltpu.VMEM((ring, 2, panel_rows, rank), bf16),
            pltpu.VMEM((chips, owned, link_rows), bf16),
            pltpu.VMEM((chips, 2, owned, link_rows), bf16),
            pltpu.VMEM((chips, 2, owned, link_rows), bf16),
            pltpu.VMEM((chips, 2, owned, rank), bf16),
            pltpu.VMEM((ring, 2, groups, owned, rank), f32),
            pltpu.VMEM((ring, groups, owned, rank), f32),
            pltpu.VMEM((ring, groups, owned, rank), bf16),
            pltpu.VMEM((chips, owned, rank), bf16),
            pltpu.VMEM((user_count, 2 * side), bf16),
            pltpu.VMEM((user_count, rank), f32),
            pltpu.VMEM((owned, rank), f32),
            pltpu.VMEM((link_rows, rank), f32),
            pltpu.SMEM((places,), jnp.int32),
            pltpu.SemaphoreType.DMA((12,)),
            pltpu.SemaphoreType.DMA((8,)),
            pltpu.SemaphoreType.DMA((8,)),
            pltpu.SemaphoreType.DMA((item_tiles // 2,)),
        ],
        compiler_params=pltpu.CompilerParams(
            collective_id=0, has_side_effects=True, vmem_limit_bytes=VMEM_BYTES
        ),
    )(*operands)
    new_users, new_items, new_link = pl.pallas_call(
        place_kernel,
        out_shape=shapes,
        in_specs=[hbm] * 3,
        out_specs=(hbm, hbm, hbm),
        scratch_shapes=[pltpu.VMEM(x.shape, f32) for x in shapes]
        + [pltpu.SemaphoreType.DMA((10,)), pltpu.SemaphoreType.DMA((10,))],
        compiler_params=pltpu.CompilerParams(vmem_limit_bytes=VMEM_BYTES),
    )(*outs)
    return (new_users, new_items[None], new_link)


def solution(mesh):
    in_specs = (
        P(("grp", "mem"), None),
        P("mem", None),
        P(),
        P("mem", "grp", None),
        P(("grp", "mem"), None, None),
        P(("grp", "mem")),
        P(("grp", "mem")),
        P(("grp", "mem")),
        P(("grp", "mem"), None),
        P("mem", "grp", None),
        P(("grp", "mem"), None),
    )
    out_specs = (P(("grp", "mem"), None), P("mem", "grp", None), P(("grp", "mem"), None))
    return jax.shard_map(
        per_device, mesh=mesh, in_specs=in_specs, out_specs=out_specs, check_vma=False
    )
```

```python
import functools

import jax
import jax.numpy as jnp
from jax import lax
from jax.experimental import pallas as pl
from jax.experimental.pallas import tpu as pltpu
from jax.sharding import PartitionSpec as P

rate_user = 0.004
prior_user = 0.5
rate_item = 0.002
prior_item = 0.2
rate_link = 0.002
prior_link = 0.5
noise_scale = 0.1

f32 = jnp.float32
bf16 = jnp.bfloat16
MESH = pl.DeviceIdType.MESH
VMEM_BYTES = 60 * 1024 * 1024


def kernel(
    groups,
    members,
    wide_cut,
    slot_place,
    live_slots,
    scales,
    panel_hbm,
    cut_hbm,
    item_noise_hbm,
    link_noise_hbm,
    feats_hbm,
    users_hbm,
    weights_hbm,
    tiles_hbm,
    noise_hbm,
    new_users,
    new_items,
    new_link,
    panel,
    cut,
    item_noise,
    link_noise,
    feats,
    users,
    weights,
    tiles,
    noise,
    items,
    feat_out,
    feat_pair,
    feat_all,
    resid_all,
    grad_part,
    grad_in,
    grad_send,
    grad_all,
    errors,
    user_sum,
    item_out,
    link_out,
    slot_of,
    local_sem,
    send_sem,
    recv_sem,
    part_sem,
):
    n = groups * members
    ring = members // 2
    chips = n // 2
    grp = lax.axis_index("grp")
    mem = lax.axis_index("mem")
    core = lax.rem(mem, 2)
    other = 1 - core
    spot = mem // 2
    chip = grp * ring + spot
    me = grp * members + mem
    panel_rows, rank = panel.shape
    owned = feats.shape[0]
    link_rows = link_noise.shape[0]
    side = tiles.shape[1]
    user_tiles = users.shape[0] // side
    item_tiles = members * panel_rows // side
    sibling = {"grp": grp, "mem": spot * 2 + other}

    def load(source, target, k):
        return pltpu.make_async_copy(source, target, local_sem.at[k])

    loads = [
        load(panel_hbm, panel, 0),
        load(feats_hbm, feats, 1),
        load(weights_hbm, weights, 2),
        None if wide_cut else load(cut_hbm, cut, 3),
        load(users_hbm, users, 4),
        load(tiles_hbm, tiles, 5),
        load(noise_hbm, noise, 6),
        load(link_noise_hbm, link_noise, 7),
        load(item_noise_hbm, item_noise, 8),
    ]
    for one in loads:
        if one is not None:
            one.start()

    def mate(q):
        return {"grp": q // ring, "mem": lax.rem(q, ring) * 2 + core}

    def send(source, target, k, device):
        pltpu.make_async_remote_copy(
            src_ref=source,
            dst_ref=target,
            send_sem=send_sem.at[k],
            recv_sem=recv_sem.at[k],
            device_id=device,
            device_id_type=MESH,
        ).start()

    def wait_for(part, sem):
        pltpu.make_async_copy(part, part, sem).wait()

    barrier = pltpu.get_barrier_semaphore()
    pl.semaphore_signal(barrier, inc=1, device_id=sibling, device_id_type=MESH)

    def greet(k, carry):
        q = lax.rem(chip + k, chips)
        pl.semaphore_signal(barrier, inc=1, device_id=mate(q), device_id_type=MESH)
        return carry

    lax.fori_loop(1, chips, greet, 0)

    slots = tiles.shape[0]
    step = 8 if slots % 8 == 0 else 1
    live_count = live_slots[0]

    def find(q, carry):
        def look(k, best):
            for j in range(step):
                at = k * step + j
                best = jnp.where((slot_place[at] == q) & (at < live_count), at, best)
            return best

        best = jnp.int32(-1)
        if slots <= 32:
            for k in range(slots // step):
                best = look(k, best)
        else:
            best = lax.fori_loop(0, slots // step, look, best)
        slot_of[q] = best
        return carry

    lax.fori_loop(0, user_tiles * item_tiles, find, 0)

    loads[0].wait()
    items[spot, core] = panel[...]
    loads[1].wait()
    if not wide_cut:
        loads[3].wait()

    def piece(d):
        if wide_cut:
            return feats[:, pl.ds(pl.multiple_of(d * link_rows, link_rows), link_rows)]
        return cut[d]

    def pack(q, carry):
        feat_pair[q, core] = piece(q * 2 + core)
        feat_out[q] = piece(q * 2 + other)
        return carry

    lax.fori_loop(0, chips, pack, 0)
    pl.semaphore_wait(barrier, chips)

    def send_panel(k, carry):
        q = lax.rem(spot + k, ring)
        send(panel, items.at[spot, core], 0, {"grp": grp, "mem": q * 2 + core})
        return carry

    lax.fori_loop(1, ring, send_panel, 0)
    send(feat_out, feat_pair.at[:, core], 1, sibling)

    loads[2].wait()
    start = pl.multiple_of(grp * owned, owned)
    own_items = panel[pl.ds(start, owned), :].astype(f32)
    resid = own_items - jnp.dot(feats[...], weights[...], preferred_element_type=f32)
    resid_all[chip, core] = resid.astype(bf16)

    def send_resid(k, carry):
        q = lax.rem(chip + k, chips)
        send(resid_all.at[chip, core], resid_all.at[chip, core], 2, mate(q))
        return carry

    lax.fori_loop(1, chips, send_resid, 0)

    wait_for(feat_out, recv_sem.at[1])
    feat_all[chip] = feat_pair[chip]

    def send_feat(k, carry):
        q = lax.rem(chip + k, chips)
        send(feat_pair.at[q], feat_all.at[chip], 4, mate(q))
        return carry

    lax.fori_loop(1, chips, send_feat, 0)

    wait_for(items.at[pl.ds(0, ring - 1), 0], recv_sem.at[0])
    send(items.at[:, core], items.at[:, core], 3, sibling)

    loads[4].wait()
    loads[5].wait()
    wait_for(items.at[:, other], recv_sem.at[3])

    wide = 2
    tall = 2 if user_tiles % 2 == 0 else 1
    chunk = wide * side
    spots_in = chunk // panel_rows // 2

    def do_chunk(c, first):
        block = items[pl.ds(c * spots_in, spots_in)].reshape(chunk, rank)
        for t in range(user_tiles // tall):
            rows = pl.ds(t * tall * side, tall * side)
            predicted = lax.dot_general(
                users[rows, :], block, (((1,), (1,)), ((), ())), preferred_element_type=f32
            )
            for a in range(tall):
                for b in range(wide):
                    slot = slot_of[(t * tall + a) * item_tiles + c * wide + b]
                    at = jnp.maximum(slot, 0)
                    live = (slot >= 0).astype(f32)
                    rating = scales[at] * tiles[at].astype(f32)
                    part = predicted[a * side : (a + 1) * side, b * side : (b + 1) * side]
                    errors[pl.ds((t * tall + a) * side, side), b * side : (b + 1) * side] = (
                        (rating - part) * live
                    ).astype(bf16)
            term = jnp.dot(errors[rows, :], block, preferred_element_type=f32)
            if first:
                user_sum[rows, :] = term
            else:
                user_sum[rows, :] += term
        grads = lax.dot_general(
            errors[...], users[...], (((0,), (0,)), ((), ())), preferred_element_type=f32
        )
        span = pl.ds(c * spots_in, spots_in)
        grad_part[span] = grads.reshape(spots_in, 2, groups, owned, rank)
        pltpu.make_async_remote_copy(
            src_ref=grad_part.at[span, other],
            dst_ref=grad_in.at[span],
            send_sem=send_sem.at[5],
            recv_sem=part_sem.at[c],
            device_id=sibling,
            device_id_type=MESH,
        ).start()

    def finish(c):
        span = pl.ds(c * spots_in, spots_in)
        wait_for(grad_in.at[span], part_sem.at[c])
        grad_send[span] = (grad_part[span, core] + grad_in[span]).astype(bf16)

        def send_grad(j, carry):
            at = lax.rem(j + chip, spots_in * groups)
            to = c * spots_in + at // groups
            g = lax.rem(at, groups)

            @pl.when(g * ring + to != chip)
            def _():
                send(
                    grad_send.at[to, g],
                    grad_all.at[chip],
                    6,
                    {"grp": g, "mem": to * 2 + core},
                )

            return carry

        lax.fori_loop(0, spots_in * groups, send_grad, 0)

    chunks = item_tiles // wide
    do_chunk(0, True)
    wait_for(resid_all.at[pl.ds(0, chips - 1), 0], recv_sem.at[2])
    send(resid_all.at[:, core], resid_all.at[:, core], 7, sibling)
    if chunks <= 4:
        for c in range(1, chunks):
            do_chunk(c, False)
            finish(c - 1)
    else:

        def later(c, carry):
            do_chunk(c, False)
            finish(c - 1)
            return carry

        lax.fori_loop(1, chunks, later, 0)

    loads[6].wait()
    for t in range(user_tiles):
        rows = pl.ds(t * side, side)
        user_sum[rows, :] = (
            (1.0 - prior_user) * users[rows, :].astype(f32)
            + rate_user * user_sum[rows, :]
            + noise_scale * noise[rows, :].astype(f32)
        )
    stores = [load(user_sum, new_users, 9)]
    stores[0].start()
    finish(chunks - 1)

    loads[7].wait()
    wait_for(feat_all.at[pl.ds(0, chips - 1)], recv_sem.at[4])
    wait_for(resid_all.at[:, other], recv_sem.at[7])
    link_sum = lax.dot_general(
        feat_all[...].reshape(n * owned, link_rows),
        resid_all[...].reshape(n * owned, rank),
        (((0,), (0,)), ((), ())),
        preferred_element_type=f32,
    )
    old_link = weights[pl.ds(pl.multiple_of(me * link_rows, link_rows), link_rows), :].astype(f32)
    link_out[...] = (
        (1.0 - prior_link) * old_link
        + rate_link * link_sum
        + noise_scale * link_noise[...].astype(f32)
    )
    stores.append(load(link_out, new_link, 10))
    stores[1].start()

    loads[8].wait()
    grad_all[chip] = grad_send[spot, grp]
    wait_for(grad_all.at[pl.ds(0, chips - 1)], recv_sem.at[6])

    def gather(k, total):
        return total + jnp.sum(grad_all[pl.ds(k * 8, 8)].astype(f32), axis=0)

    item_sum = lax.fori_loop(0, chips // 8, gather, jnp.zeros((owned, rank), f32))
    item_out[...] = (
        own_items
        + rate_item * item_sum
        - prior_item * resid
        + noise_scale * item_noise[...].astype(f32)
    )
    stores.append(load(item_out, new_items, 11))
    stores[2].start()

    wait_for(items.at[pl.ds(0, ring - 1), 0], send_sem.at[0])
    wait_for(feat_out, send_sem.at[1])
    wait_for(resid_all.at[pl.ds(0, chips - 1), 0], send_sem.at[2])
    wait_for(items.at[:, 0], send_sem.at[3])
    wait_for(feat_all.at[pl.ds(0, chips - 1)], send_sem.at[4])
    wait_for(grad_in, send_sem.at[5])
    wait_for(grad_all.at[pl.ds(0, chips - 1)], send_sem.at[6])
    wait_for(resid_all.at[:, 0], send_sem.at[7])
    for one in stores:
        one.wait()


def place_kernel(a, b, c, x, y, z, held_a, held_b, held_c, in_sem, out_sem):
    pieces = 8
    rows = a.shape[0] // pieces
    paths = [(b, held_b, y), (c, held_c, z)]
    for k in range(pieces):
        part = pl.ds(k * rows, rows)
        paths.append((a.at[part], held_a.at[part], x.at[part]))
    ins = [
        pltpu.make_async_copy(source, held, in_sem.at[k])
        for k, (source, held, target) in enumerate(paths)
    ]
    outs = [
        pltpu.make_async_copy(held, target, out_sem.at[k])
        for k, (source, held, target) in enumerate(paths)
    ]
    for copy in ins:
        copy.start()
    for first, second in zip(ins, outs):
        first.wait()
        second.start()
    for copy in outs:
        copy.wait()


def per_device(
    user_factors,
    item_factors,
    link_weights,
    item_feat,
    tile_values,
    tile_scale,
    tile_place,
    tile_count,
    user_noise,
    item_noise,
    link_noise,
):
    groups = lax.axis_size("grp")
    members = lax.axis_size("mem")
    n = groups * members
    slots, side, unused = tile_values.shape
    user_count, rank = user_factors.shape
    panel_rows = item_factors.shape[0]
    owned = item_feat.shape[1]
    features = item_feat.shape[2]
    link_rows = link_noise.shape[0]
    places = (user_count // side) * (panel_rows * members // side)
    feats = item_feat[0]

    smem = pl.BlockSpec(memory_space=pltpu.SMEM)
    hbm = pl.BlockSpec(memory_space=pl.ANY)
    wide_cut = link_rows % 128 == 0
    if wide_cut:
        cut = item_noise[0]
    else:
        cut = feats.reshape(owned, n, link_rows).transpose(1, 0, 2)
    operands = [
        tile_place,
        tile_count,
        tile_scale,
        item_factors,
        cut,
        item_noise[0],
        link_noise,
        feats,
        user_factors,
        link_weights,
        tile_values,
        user_noise,
    ]
    ring = members // 2
    chips = n // 2
    item_tiles = panel_rows * members // side
    shapes = (
        jax.ShapeDtypeStruct((user_count, rank), f32),
        jax.ShapeDtypeStruct((owned, rank), f32),
        jax.ShapeDtypeStruct((link_rows, rank), f32),
    )
    outs = pl.pallas_call(
        functools.partial(kernel, groups, members, wide_cut),
        out_shape=shapes,
        in_specs=[smem, smem, smem] + [hbm] * 9,
        out_specs=(hbm, hbm, hbm),
        scratch_shapes=[pltpu.VMEM(x.shape, bf16) for x in operands[3:]]
        + [
            pltpu.VMEM((ring, 2, panel_rows, rank), bf16),
            pltpu.VMEM((chips, owned, link_rows), bf16),
            pltpu.VMEM((chips, 2, owned, link_rows), bf16),
            pltpu.VMEM((chips, 2, owned, link_rows), bf16),
            pltpu.VMEM((chips, 2, owned, rank), bf16),
            pltpu.VMEM((ring, 2, groups, owned, rank), f32),
            pltpu.VMEM((ring, groups, owned, rank), f32),
            pltpu.VMEM((ring, groups, owned, rank), bf16),
            pltpu.VMEM((chips, owned, rank), bf16),
            pltpu.VMEM((user_count, 2 * side), bf16),
            pltpu.VMEM((user_count, rank), f32),
            pltpu.VMEM((owned, rank), f32),
            pltpu.VMEM((link_rows, rank), f32),
            pltpu.SMEM((places,), jnp.int32),
            pltpu.SemaphoreType.DMA((12,)),
            pltpu.SemaphoreType.DMA((8,)),
            pltpu.SemaphoreType.DMA((8,)),
            pltpu.SemaphoreType.DMA((item_tiles // 2,)),
        ],
        compiler_params=pltpu.CompilerParams(
            collective_id=0, has_side_effects=True, vmem_limit_bytes=VMEM_BYTES
        ),
    )(*operands)
    new_users, new_items, new_link = pl.pallas_call(
        place_kernel,
        out_shape=shapes,
        in_specs=[hbm] * 3,
        out_specs=(hbm, hbm, hbm),
        scratch_shapes=[pltpu.VMEM(x.shape, f32) for x in shapes]
        + [pltpu.SemaphoreType.DMA((10,)), pltpu.SemaphoreType.DMA((10,))],
        compiler_params=pltpu.CompilerParams(vmem_limit_bytes=VMEM_BYTES),
    )(*outs)
    return (new_users, new_items[None], new_link)


def solution(mesh):
    in_specs = (
        P(("grp", "mem"), None),
        P("mem", None),
        P(),
        P("mem", "grp", None),
        P(("grp", "mem"), None, None),
        P(("grp", "mem")),
        P(("grp", "mem")),
        P(("grp", "mem")),
        P(("grp", "mem"), None),
        P("mem", "grp", None),
        P(("grp", "mem"), None),
    )
    out_specs = (P(("grp", "mem"), None), P("mem", "grp", None), P(("grp", "mem"), None))
    return jax.shard_map(
        per_device, mesh=mesh, in_specs=in_specs, out_specs=out_specs, check_vma=False
    )
```
